128 devices in a mesh: grp: 4 (over x), dev: 32 (over y, z, core).
Axes of the slice: x: 4, y: 4, z: 4, core: 2. Of those that a mesh axis runs over, the one named last changes fastest.
Arguments:
- load: float32 [1024, 1024, 128], P('grp', 'dev'), may hold values from -11 to 11
- east_class: int32 [1024, 1024], P('grp', 'dev'), may hold values from 0 to 7
- north_class: int32 [1024, 1024], P('grp', 'dev'), may hold values from 0 to 7
- cond_table: float32 [8], replicated, may hold values from 0.25 to 4
- taps: int32 [128, 16], replicated, may hold values from 0 to 1048575
- tap_current: float32 [128, 16], replicated, may hold values from -16 to 16
Outputs:
- potential: float32 [1024, 1024, 128], P('grp', 'dev')
The draws below stay inside these ranges and needn't reach their ends.
Inputs may be any that keep to these rules, and one draw needn't show every extreme that they name: `taps`: tap number i * 1024 + j stands for node (i, j).
All inputs are finite; a program needn't handle non-finite values.
Results may differ from the reference program's by a relative error of at most 0.0001.
Values sent between devices are 32-bit elements; how exact they have to be, the bound alone decides.
A program may use at most 128 MiB of HBM per device.

```python
import math
import jax
import jax.numpy as jnp
from jax import lax

C = 128
CLASSES = 8
TAPS = 16
LEVELS = 5
NX = 1024
NY = 1024


def draw_load(key, part):
    first_key = jax.random.fold_in(jax.random.fold_in(key, 17), 0)
    rough = 1.5 * jnp.clip(jax.random.normal(first_key, (NX, NY, C), jnp.float32), -4.0, 4.0)
    return rough


def with_ends(entries, stream_key, low, high):
    index_at = [jax.random.randint(jax.random.fold_in(stream_key, axis), (), 0, length) for axis, length in enumerate(entries.shape)]
    main_axis = entries.shape.index(max(entries.shape))
    beside = index_at[:main_axis] + [(index_at[main_axis] + 1) % entries.shape[main_axis]] + index_at[main_axis + 1:]
    return entries.at[tuple(index_at)].set(low).at[tuple(beside)].set(high)


def bell_draw(rng, extent, scale, reach, kind=jnp.bfloat16):
    drawn = scale * jax.random.normal(rng, extent, jnp.float32)
    return jnp.clip(drawn, min=-reach, max=reach).astype(kind)


def setup_inputs(seed: int = 0) -> dict:
    arg_keys = jax.random.split(jax.random.key(seed), 7)
    return {
        "load": draw_load(jax.random.fold_in(arg_keys[6], 71), 0),
        "east_class": with_ends(jax.random.randint(arg_keys[1], (NX, NY), 0, CLASSES), jax.random.fold_in(arg_keys[1], 1), 0, CLASSES - 1).astype(jnp.int32),
        "north_class": with_ends(jax.random.randint(arg_keys[2], (NX, NY), 0, CLASSES), jax.random.fold_in(arg_keys[2], 1), 0, CLASSES - 1).astype(jnp.int32),
        "cond_table": jnp.clip(jnp.exp(jax.random.uniform(arg_keys[3], (CLASSES,), jnp.float32, math.log(0.25), math.log(4.0))), 0.25, 4.0),
        "taps": with_ends(jax.random.randint(arg_keys[4], (C, TAPS), 0, NX * NY), jax.random.fold_in(arg_keys[4], 1), 0, (NX * NY) - 1).astype(jnp.int32),
        "tap_current": bell_draw(arg_keys[5], (C, TAPS), 4.0, 16.0, jnp.float32),
    }


RELAXATION = 0.8
SHUNT_CONDUCT = 0.01

def diagonal_of(east_cond, north_cond, shunt):
    west_cond = jnp.pad(east_cond, ((1, 0), (0, 0)))[:-1]
    south_cond = jnp.pad(north_cond, ((0, 0), (1, 0)))[:, :-1]
    return shunt + east_cond + west_cond + north_cond + south_cond

def operate(potential, east_cond, north_cond, shunt):
    padded = jnp.pad(potential, ((1, 1), (1, 1), (0, 0)))
    west_cond = jnp.pad(east_cond, ((1, 0), (0, 0)))[:-1]
    south_cond = jnp.pad(north_cond, ((0, 0), (1, 0)))[:, :-1]
    diagonal = shunt + east_cond + west_cond + north_cond + south_cond
    applied = diagonal[..., None] * potential - east_cond[..., None] * padded[2:, 1:-1] - west_cond[..., None] * padded[:-2, 1:-1] - north_cond[..., None] * padded[1:-1, 2:] - south_cond[..., None] * padded[1:-1, :-2]
    return (applied, diagonal)

def relax(potential, source, east_cond, north_cond, shunt):
    applied, diagonal = operate(potential, east_cond, north_cond, shunt)
    return potential + RELAXATION * (source - applied) / diagonal[..., None]

def restrict(values):
    row_count, col_count, cand_count = values.shape
    return values.reshape(row_count // 2, 2, col_count // 2, 2, cand_count).sum(axis=(1, 3))

def prolong(values):
    return jnp.repeat(jnp.repeat(values, 2, axis=0), 2, axis=1)

def coarsen(east_cond, north_cond):
    row_count, col_count = east_cond.shape
    coarse_east = east_cond.reshape(row_count // 2, 2, col_count // 2, 2)[:, 1].sum(axis=-1)
    coarse_north = north_cond.reshape(row_count // 2, 2, col_count // 2, 2)[:, :, :, 1].sum(axis=1)
    return (coarse_east, coarse_north)

def coarse_factor(east_cond, north_cond, shunt):
    row_count, col_count = east_cond.shape
    node_count = row_count * col_count
    diagonal = diagonal_of(east_cond, north_cond, shunt).reshape(-1)
    east_flat = east_cond.reshape(-1)
    north_flat = north_cond.reshape(-1)
    matrix = jnp.diag(diagonal) - jnp.diag(east_flat[:node_count - col_count], col_count) - jnp.diag(east_flat[:node_count - col_count], -col_count) - jnp.diag(north_flat[:node_count - 1], 1) - jnp.diag(north_flat[:node_count - 1], -1)
    return jnp.linalg.cholesky(matrix)

def vcycle(source, conduct_list, factor):
    stored = []
    for height in range(LEVELS):
        east_cond, north_cond = conduct_list[height]
        shunt = SHUNT_CONDUCT * 4.0 ** height
        diagonal = diagonal_of(east_cond, north_cond, shunt)
        initial = RELAXATION * source / diagonal[..., None]
        potential = relax(initial, source, east_cond, north_cond, shunt)
        applied = operate(potential, east_cond, north_cond, shunt)[0]
        stored.append((potential, source))
        source = restrict(source - applied)
    row_count, col_count = conduct_list[LEVELS][0].shape
    correction = jax.scipy.linalg.cho_solve((factor, True), source.reshape(row_count * col_count, -1))
    correction = correction.reshape(row_count, col_count, -1)
    for height in reversed(range(LEVELS)):
        east_cond, north_cond = conduct_list[height]
        shunt = SHUNT_CONDUCT * 4.0 ** height
        potential, source = stored[height]
        potential = potential + prolong(correction)
        for iteration in range(2):
            potential = relax(potential, source, east_cond, north_cond, shunt)
        correction = potential
    return correction

def reference(load, east_class, north_class, cond_table, taps, tap_current):
    east_cond = cond_table[east_class].at[-1, :].set(0.0)
    north_cond = cond_table[north_class].at[:, -1].set(0.0)
    conduct_list = [(east_cond, north_cond)]
    for height in range(LEVELS):
        conduct_list.append(coarsen(*conduct_list[-1]))
    factor = coarse_factor(*conduct_list[LEVELS], SHUNT_CONDUCT * 4.0 ** LEVELS)
    per_block = 16

    def solve_block(block_index):
        offset = block_index * per_block
        block_load = lax.dynamic_slice_in_dim(load, offset, per_block, 2)
        block_taps = lax.dynamic_slice_in_dim(taps, offset, per_block, 0)
        block_amps = lax.dynamic_slice_in_dim(tap_current, offset, per_block, 0)
        columns = jnp.broadcast_to(jnp.arange(per_block, dtype=jnp.int32)[:, None], block_taps.shape)
        injected = jnp.zeros((NX * NY, per_block), load.dtype).at[block_taps, columns].add(block_amps)
        source = injected.reshape(NX, NY, per_block) - block_load
        return vcycle(source, conduct_list, factor)
    solved = lax.map(solve_block, jnp.arange(C // per_block, dtype=jnp.int32))
    return jnp.moveaxis(solved, 0, 2).reshape(NX, NY, C)
```

```python
import functools

import jax
import jax.numpy as jnp
from jax import lax
from jax.experimental import pallas as pl
from jax.experimental.pallas import tpu as pltpu
from jax.sharding import PartitionSpec as P

MESH = pl.DeviceIdType.MESH
HI = lax.Precision.HIGHEST
F32 = jnp.float32
LEVELS = 5
SHUNT = 0.01
RELAX = 0.8
LANES = 128

HALO = {1: 4, 2: 5, 3: 5, 4: 5}
WIDTH = {1: 24, 2: 24, 3: 16, 4: 16}
OFFSET = {1: 4, 2: 8, 3: 6, 4: 6}
PACK_E = {1: 0, 2: 32, 3: 48, 4: 56}
PACK_N = {1: 16, 2: 40, 3: 52, 4: 58}
PACK_ROWS = 64
MARGIN = 8
REACH = 3


def dot(a, b, dims=((1,), (0,))):
    return lax.dot_general(a, b, (dims, ((), ())), precision=HI, preferred_element_type=F32)


def iota(shape, dim):
    return lax.broadcasted_iota(jnp.int32, shape, dim)


def rows_loop(lo, hi, fn, unroll=1):
    def step(i, carry):
        fn(i)
        return carry

    lax.fori_loop(lo, hi, step, 0, unroll=unroll)


def source_kernel(block_rows, hit_ref, load_ref, rows_ref, cols_ref, cur_ref, out_ref):
    out_ref[...] = -load_ref[...]
    base = pl.program_id(0) * block_rows
    width = load_ref.shape[1]
    col_ids = iota((width, LANES), 0)

    def one(r, carry):
        @pl.when(hit_ref[base + r] > 0)
        def _():
            here = jnp.where(rows_ref[...] == base + r, cur_ref[...], 0.0)
            total = jnp.zeros((width, LANES), F32)
            for k in range(rows_ref.shape[0]):
                total += jnp.where(cols_ref[k : k + 1] == col_ids, here[k : k + 1], 0.0)
            out_ref[r] = out_ref[r] + total

        return carry

    lax.fori_loop(0, block_rows, one, 0)


def around(dist):
    return [
        (di, dd)
        for di in (-1, 0, 1)
        for dd in range(-dist, dist + 1)
        if (di, dd) != (0, 0)
    ]


def overlap(step, size, halo):
    low = max(0, step * size - halo)
    high = min(size, step * size + size + halo)
    return low, high - low


def cycle_kernel(
    n_grp, n_dev, n_rows, n_cols,
    src_hbm, east_ref, north_ref, tab_ref,
    out_hbm,
    s0, u0, v0, e0, n0, w0, nt_ext, pack,
    s1, s2, s3, s4, u1, u2, u3, u4, v1, v2, v3, v4,
    e1, e2, e3, e4, n1, n2, n3, n4, w1, w2, w3, w4,
    cx1, cx2, cx3, cx4,
    g_cond, g_src, x_ext, c5,
    m1, m2, m3, m4, m5, y1, y2, y3, y4, y5, t1, t2, t3, t4, t5, p1, p2, p3, p4, p5, p6,
    send, recv, local,
):
    g = lax.axis_index("grp")
    d = lax.axis_index("dev")
    S = {1: s1, 2: s2, 3: s3, 4: s4}
    U = {0: u0, 1: u1, 2: u2, 3: u3, 4: u4}
    V = {0: v0, 1: v1, 2: v2, 3: v3, 4: v4}
    E = {0: e0, 1: e1, 2: e2, 3: e3, 4: e4}
    N = {0: n0, 1: n1, 2: n2, 3: n3, 4: n4}
    W = {0: w0, 1: w1, 2: w2, 3: w3, 4: w4}
    CX = {1: cx1, 2: cx2, 3: cx3, 4: cx4}
    S[0] = s0
    MT = {1: m1, 2: m2, 3: m3, 4: m4, 5: m5}
    YY = {1: y1, 2: y2, 3: y3, 4: y4, 5: y5}
    YT = {1: t1, 2: t2, 3: t3, 4: t4, 5: t5}
    PP = {1: p1, 2: p2, 3: p3, 4: p4, 5: p5, 6: p6}
    R = {h: n_rows >> h for h in range(6)}
    C = {h: n_cols >> h for h in range(6)}
    H = dict(HALO)
    H[0] = 0
    JP = dict(WIDTH)
    JP[0] = n_cols
    OJ = dict(OFFSET)
    OJ[0] = 0

    counter = [0]

    def take():
        counter[0] += 1
        return counter[0] - 1

    def at(di, dd):
        return (lax.rem(g + (di + n_grp), n_grp), lax.rem(d + (dd + n_dev), n_dev))

    def remote(src, dst, device):
        m = take()
        return pltpu.make_async_remote_copy(
            src_ref=src, dst_ref=dst, send_sem=send.at[m], recv_sem=recv.at[m],
            device_id=device, device_id_type=MESH,
        )

    zd = lax.rem(d, 8)
    yd = d // 8
    near = [(o, (g, yd * 8 + lax.rem(zd + o, 8))) for o in range(1, 8)]
    far = [
        (lax.rem(g + a, n_grp), lax.rem(yd + b, 4) * 8 + zd)
        for a in range(n_grp)
        for b in range(4)
        if (a, b) != (0, 0)
    ]
    partners = [at(di, dd) for di, dd in around(REACH)] + [dev for _, dev in near] + far

    barrier = pltpu.get_barrier_semaphore()
    for dev in partners:
        pl.semaphore_signal(barrier, inc=1, device_id=dev, device_id_type=MESH)

    own_rows = pl.ds(0, n_rows)
    fetch = pltpu.make_async_copy(src_hbm, s0, local.at[0])
    fetch.start()

    def conductance(cls):
        value = jnp.full(cls.shape, tab_ref[0], F32)
        for c in range(1, 8):
            value = jnp.where(cls == c, tab_ref[c], value)
        return value

    rows_c = iota((n_rows, n_cols), 0)
    cols_c = iota((n_rows, n_cols), 1)
    east = conductance(east_ref[...])
    east = jnp.where((rows_c == n_rows - 1) & (g == n_grp - 1), 0.0, east)
    north = conductance(north_ref[...])
    north = jnp.where((cols_c == n_cols - 1) & (d == n_dev - 1), 0.0, north)
    et = east.T
    nt = north.T
    nt_ext[pl.ds(MARGIN, n_cols), :] = nt

    packed = jnp.zeros((PACK_ROWS, LANES), F32)
    ri = iota((n_rows, LANES), 0)
    li = iota((n_rows, LANES), 1)
    pr = iota((PACK_ROWS, n_cols), 0)
    pj = iota((PACK_ROWS, n_cols), 1)
    for h in range(1, LEVELS):
        f = 1 << h
        last = jnp.where(ri == li * f + (f - 1), 1.0, 0.0)
        every = jnp.where(ri // f == li, 1.0, 0.0)
        qe = dot(et, last)
        qn = dot(nt, every)
        re, rn = pr - PACK_E[h], pr - PACK_N[h]
        pick_e = jnp.where((re >= 0) & (re < C[h]) & (pj // f == re), 1.0, 0.0)
        pick_n = jnp.where((rn >= 0) & (rn < C[h]) & (pj == rn * f + (f - 1)), 1.0, 0.0)
        packed += dot(pick_e, qe) + dot(pick_n, qn)
    pack[1, REACH] = packed

    si = iota((R[5], n_rows), 0)
    ci = iota((R[5], n_rows), 1)
    fe = jnp.where(ci == si * 32 + 31, 1.0, 0.0)
    fn_ = jnp.where(ci // 32 == si, 1.0, 0.0)
    e5 = jnp.sum(dot(fe, east), axis=1, keepdims=True)
    n5s = dot(fn_, north)
    n5 = jnp.sum(jnp.where(iota(n5s.shape, 1) == n_cols - 1, n5s, 0.0), axis=1, keepdims=True)
    both = jnp.where(iota((R[5], LANES), 1) < 64, e5, n5)
    mine8 = pl.ds(pl.multiple_of(g * 8, 8), 8)
    g_cond[d, mine8, :] = both

    pl.semaphore_wait(barrier, len(partners))

    def gather_near(buf):
        return [
            remote(buf.at[d, mine8, :], buf.at[d, mine8, :], dev) for _, dev in near
        ]

    def gather_far(buf):
        slab = pl.ds(pl.multiple_of(yd * 8, 8), 8)
        return [remote(buf.at[slab, mine8, :], buf.at[slab, mine8, :], dev) for dev in far]

    def start(copies):
        for c in copies:
            c.start()

    def wait(copies):
        for c in copies:
            c.wait()

    north_edge = [
        remote(nt_ext.at[pl.ds(MARGIN + n_cols - 1, 1), :], nt_ext.at[pl.ds(MARGIN - 1, 1), :], at(0, 1))
    ]
    start(north_edge)
    cond_near = gather_near(g_cond)
    start(cond_near)
    pack_copies = []
    for di, dd in around(REACH):
        lo = {0: 0, 1: 0, 2: 48, 3: 56}[abs(dd)]
        part = pl.ds(lo, PACK_ROWS - lo)
        pack_copies.append(
            remote(pack.at[1, REACH, part, :], pack.at[1 - di, REACH - dd, part, :], at(di, dd))
        )
    start(pack_copies)

    def spread(block, lane, width):
        ids = iota(block.shape, 1)
        col = jnp.sum(jnp.where(ids == lane, block, 0.0), axis=1, keepdims=True)
        return jnp.broadcast_to(col, (width, LANES))

    for half in range(n_rows // LANES):
        blk = et[:, half * LANES : (half + 1) * LANES]

        def fill(i, blk=blk, half=half):
            e0[half * LANES + i + 1] = spread(blk, i, n_cols)

        rows_loop(0, LANES, fill, unroll=4)
    east_edge = [remote(e0.at[n_rows], e0.at[0], at(1, 0))]
    start(east_edge)
    wait(north_edge)
    for half in range(n_rows // LANES):
        blk = nt_ext[:, half * LANES : (half + 1) * LANES]

        def fill(i, blk=blk, half=half):
            n0[half * LANES + i + 1] = spread(blk, i, n_cols + MARGIN)

        rows_loop(0, LANES, fill, unroll=4)

    wait(cond_near)
    cond_far = gather_far(g_cond)
    start(cond_far)
    wait(east_edge)

    def win(h, shift=0):
        return pl.ds(MARGIN + shift, JP[h])

    def diagonal(h, r, shunt):
        return shunt + E[h][r] + E[h][r - 1] + N[h][r, win(h), :] + N[h][r, win(h, -1), :]

    def around_sum(h, ref, r):
        return (
            E[h][r] * ref[r + 1, win(h), :]
            + E[h][r - 1] * ref[r - 1, win(h), :]
            + N[h][r, win(h), :] * ref[r, win(h, 1), :]
            + N[h][r, win(h, -1), :] * ref[r, win(h, -1), :]
        )

    def set_weights(h):
        shunt = SHUNT * 4.0**h

        def fill(r):
            W[h][r] = RELAX / diagonal(h, r, shunt)

        rows_loop(1, R[h] + 2 * H[h] + 1, fill, unroll=2)

    def s_row(h, r):
        return s0[r - 1] if h == 0 else S[h][r]

    def first(h):
        def fill(r):
            U[h][r, win(h), :] = W[h][r] * s_row(h, r)

        rows_loop(1, R[h] + 2 * H[h] + 1, fill, unroll=2)

    def presmooth(h):
        lo = 1 if h == 0 else 2

        def fill(r):
            V[h][r, win(h), :] = W[h][r] * (1.2 * s_row(h, r) + around_sum(h, U[h], r))

        rows_loop(lo, R[h] + 2 * H[h] + 2 - lo, fill, unroll=2)

    def restrict(h):
        shunt = SHUNT * 4.0**h

        def residual(r):
            return (
                s_row(h, r)
                + around_sum(h, V[h], r)
                - diagonal(h, r, shunt) * V[h][r, win(h), :]
            )

        base = H[h] + 1

        def fill(q):
            U[h][q, win(h), :] = residual(base + 2 * q) + residual(base + 2 * q + 1)

        rows_loop(0, R[h + 1], fill, unroll=2)
        cc = C[h + 1]

        def halve(q):
            a = U[h][q, pl.ds(MARGIN + OJ[h], cc, stride=2), :]
            b = U[h][q, pl.ds(MARGIN + OJ[h] + 1, cc, stride=2), :]
            if h == LEVELS - 1:
                g_src[d, pl.ds(g * 8 + q, 1), :] = a + b
            else:
                S[h + 1][q + H[h + 1] + 1, pl.ds(OJ[h + 1], cc), :] = a + b

        rows_loop(0, R[h + 1], halve, unroll=2)

    def edges(ref):
        rows = pl.ds(1, n_rows)
        cols = pl.ds(MARGIN, n_cols)
        return [
            remote(ref.at[rows, pl.ds(MARGIN + n_cols - 1, 1), :], ref.at[rows, pl.ds(MARGIN - 1, 1), :], at(0, 1)),
            remote(ref.at[rows, pl.ds(MARGIN, 1), :], ref.at[rows, pl.ds(MARGIN + n_cols, 1), :], at(0, -1)),
            remote(ref.at[n_rows, cols, :], ref.at[0, cols, :], at(1, 0)),
            remote(ref.at[1, cols, :], ref.at[n_rows + 1, cols, :], at(-1, 0)),
        ]

    def halos(h):
        dist = -(-H[h] // C[h])
        copies = []
        for di, dd in around(dist):
            i0, ni = overlap(di, R[h], H[h])
            j0, nj = overlap(dd, C[h], H[h])
            src = S[h].at[pl.ds(i0 + H[h] + 1, ni), pl.ds(j0 + OJ[h], nj), :]
            dst = S[h].at[
                pl.ds(i0 - di * R[h] + H[h] + 1, ni), pl.ds(j0 - dd * C[h] + OJ[h], nj), :
            ]
            copies.append(remote(src, dst, at(di, dd)))
        return copies

    set_weights(0)
    fetch.wait()
    first(0)
    u_edges = edges(u0)
    start(u_edges)

    wait(pack_copies)
    for h in range(1, LEVELS):
        width = MARGIN + JP[h]
        for t, base in ((0, PACK_E[h]), (1, PACK_N[h])):
            for di in range(3):
                for dd in range(-REACH, REACH + 1):
                    first_j = dd * C[h] + OJ[h] + MARGIN
                    lo = max(first_j, MARGIN - 1)
                    hi = min(first_j + C[h], width)
                    if hi > lo and abs(dd) <= -(-(H[h] + 1) // C[h]):
                        CX[h][t, di, pl.ds(lo, hi - lo), :] = pack[
                            di, dd + REACH, pl.ds(base + lo - first_j, hi - lo), :
                        ]

        def fill(i, di, shift, h=h, width=width):
            r = i + H[h] + 1 + shift
            E[h][r] = spread(CX[h][0, di, pl.ds(MARGIN, JP[h]), :], i, JP[h])
            N[h][r] = spread(CX[h][1, di], i, width)

        rows_loop(R[h] - H[h] - 1, R[h], functools.partial(fill, di=0, shift=-R[h]))
        rows_loop(0, R[h], functools.partial(fill, di=1, shift=0), unroll=4)
        rows_loop(0, H[h] + 1, functools.partial(fill, di=2, shift=R[h]))
        set_weights(h)

    wait(cond_far)

    nb = n_dev
    nn = n_grp * R[5]
    sub = iota((nn, nn), 0)
    lane = iota((nn, nn), 1)
    eye = sub == lane
    shunt5 = SHUNT * 4.0**LEVELS

    def coarse_block(k):
        both = g_cond[k]
        ee = both[:, :nn]
        low = pltpu.roll(both, 1, 0)[:, :nn]
        nc = pltpu.roll(both, 64, 1)[:, :nn]
        before = pltpu.roll(g_cond[(k - 1) % nb], 64, 1)[:, :nn]
        block = jnp.where(eye, shunt5 + ee + low + nc + before, 0.0)
        block = jnp.where(lane == sub + 1, -ee, block)
        block = jnp.where(lane == sub - 1, -low, block)
        return block, jnp.where(eye, -nc, 0.0), jnp.where(eye, -before, 0.0)

    def invert(ref):
        count = ref.shape[0]
        l3 = iota((count, nn, nn), 2)
        s3_ = iota((count, nn, nn), 1)
        lr = iota((count, 1, nn), 2)

        def step(k, carry):
            mat = ref[...]
            row = ref[:, pl.ds(k, 1), :]
            pivot = 1.0 / jnp.sum(jnp.where(lr == k, row, 0.0), axis=2, keepdims=True)
            col = jnp.sum(jnp.where(l3 == k, mat, 0.0), axis=2, keepdims=True)
            col = jnp.where(s3_ == k, -1.0, col)
            row = jnp.where(lr == k, pivot, row * pivot)
            ref[...] = jnp.where((l3 == k) | (s3_ == k), 0.0, mat) - col * row
            return carry

        lax.fori_loop(0, nn, step, 0)

    even = []
    for q in range(nb // 2):
        even.append(coarse_block(2 * q)[0])
        block, right, left = coarse_block(2 * q + 1)
        PP[1][q] = block
        MT[1][q] = jnp.concatenate([right, left], axis=0)
    for lev in range(1, 6):
        half = nb >> lev
        invert(PP[lev])
        zs = []
        for q in range(half):
            mt = MT[lev][q]
            inv = PP[lev][q]
            yt = dot(mt, inv)
            YT[lev][q] = yt
            YY[lev][q] = dot(inv, mt, ((1,), (1,)))
            zs.append(dot(yt, mt, ((1,), (1,))))
        new = []
        for q in range(half):
            block = even[q] - zs[q][nn:, nn:]
            if q > 0:
                block = block - zs[q - 1][:nn, :nn]
            new.append(block)
        if lev == 5:
            PP[6][0] = new[0]
        else:
            for q in range(half // 2):
                odd = 2 * q + 1
                PP[lev + 1][q] = new[odd]
                MT[lev + 1][q] = jnp.concatenate(
                    [-zs[odd][:nn, nn:], -zs[odd - 1][nn:, :nn]], axis=0
                )
            even = new[0::2]
    invert(PP[6])

    wait(u_edges)
    presmooth(0)
    v_edges = edges(v0)
    start(v_edges)
    wait(v_edges)
    restrict(0)
    for h in range(1, LEVELS):
        copies = halos(h)
        start(copies)
        wait(copies)
        first(h)
        presmooth(h)
        restrict(h)
    src_near = gather_near(g_src)
    start(src_near)
    wait(src_near)
    src_far = gather_far(g_src)
    start(src_far)
    x_ext[...] = jnp.zeros_like(x_ext)
    wait(src_far)

    for lev in range(1, 6):
        st = 1 << (lev - 1)
        for q in range(nb >> lev):
            odd = (2 * q + 1) * st
            upd = dot(YT[lev][q], g_src[odd])
            g_src[odd - st] = g_src[odd - st] - upd[nn:]
            if odd + st < nb:
                g_src[odd + st] = g_src[odd + st] - upd[:nn]
    inner = pl.ds(MARGIN, nn)
    x_ext[4, inner, :] = dot(PP[6][0], g_src[0])
    for lev in range(5, 0, -1):
        st = 1 << (lev - 1)
        for q in range(nb >> lev):
            odd = (2 * q + 1) * st
            x = dot(PP[lev][q], g_src[odd])
            y = YY[lev][q]
            x = x - dot(y[:, nn:], x_ext[4 + odd - st, inner, :])
            if odd + st < nb:
                x = x - dot(y[:, :nn], x_ext[4 + odd + st, inner, :])
            x_ext[4 + odd, inner, :] = x

    for k in range(8):
        part = x_ext[d + 1 + k, pl.ds(pl.multiple_of(g * 8, 8), 24), :]
        for i in range(12):
            c5[i, k : k + 1, :] = part[6 + i : 7 + i]

    def smooth(h, dst, ref, halo):
        lo = H[h] + 1 - halo if h else 1
        hi = R[h] + H[h] + 1 + halo if h else n_rows + 1

        def fill(r):
            dst[r, win(h), :] = 0.2 * ref[r, win(h), :] + W[h][r] * (
                s_row(h, r) + around_sum(h, ref, r)
            )

        rows_loop(lo, hi, fill, unroll=2)

    for h in range(LEVELS - 1, 0, -1):
        p = H[h] - 1
        first_q = -(-p // 2)
        size = JP[h] // 2

        def lift(q, h=h, size=size):
            if h == LEVELS - 1:
                coarse = c5[q + 2]
            else:
                cofs = MARGIN + OJ[h + 1] - OJ[h] // 2
                coarse = V[h + 1][q + H[h + 1] + 1, pl.ds(cofs, size), :]
            for a in range(2):
                r = 2 * q + a + H[h] + 1
                for b in range(2):
                    cols = pl.ds(MARGIN + b, size, stride=2)
                    V[h][r, cols, :] = V[h][r, cols, :] + coarse

        rows_loop(-first_q, R[h] // 2 + first_q, lift, unroll=2)
        smooth(h, U[h], V[h], p - 1)
        smooth(h, V[h], U[h], p - 2)

    half_cols = n_cols // 2

    def lift0(q, rows):
        coarse = V[1][q + H[1] + 1, pl.ds(MARGIN + OJ[1] - 1, half_cols + 2), :]
        for a in rows:
            r = 2 * q + a + 1
            for b in range(2):
                cols = pl.ds(MARGIN - 2 + b, half_cols + 2, stride=2)
                v0[r, cols, :] = v0[r, cols, :] + coarse

    lift0(-1, (1,))
    rows_loop(0, n_rows // 2, functools.partial(lift0, rows=(0, 1)), unroll=2)
    lift0(n_rows // 2, (0,))
    smooth(0, u0, v0, 0)
    m_edges = edges(u0)
    start(m_edges)
    wait(m_edges)

    def last(r):
        s0[r - 1] = 0.2 * u0[r, win(0), :] + W[0][r] * (s0[r - 1] + around_sum(0, u0, r))

    rows_loop(1, n_rows + 1, last, unroll=2)
    done = pltpu.make_async_copy(s0, out_hbm, local.at[0])
    done.start()
    done.wait()
    assert counter[0] <= N_COPIES, counter[0]


N_COPIES = 150


def body(n_grp, n_dev, load, east_class, north_class, cond_table, taps, tap_current):
    n_rows, n_cols, cands = load.shape
    row0 = lax.axis_index("grp") * n_rows
    col0 = lax.axis_index("dev") * n_cols
    rows = (taps // (n_dev * n_cols) - row0).T
    cols = (taps % (n_dev * n_cols) - col0).T
    inside = (cols >= 0) & (cols < n_cols)
    marked = jnp.where(inside, rows, -1).reshape(-1)
    hit = jnp.any(
        marked[None, :] == jnp.arange(n_rows, dtype=jnp.int32)[:, None], axis=1
    ).astype(jnp.int32)
    blk = 32
    whole = lambda shape: pl.BlockSpec(shape, lambda i, *_: (0,) * len(shape))
    source = pl.pallas_call(
        functools.partial(source_kernel, blk),
        grid_spec=pltpu.PrefetchScalarGridSpec(
            num_scalar_prefetch=1,
            grid=(n_rows // blk,),
            in_specs=[
                pl.BlockSpec((blk, n_cols, cands), lambda i, *_: (i, 0, 0)),
                whole(rows.shape),
                whole(rows.shape),
                whole(rows.shape),
            ],
            out_specs=pl.BlockSpec((blk, n_cols, cands), lambda i, *_: (i, 0, 0)),
        ),
        out_shape=jax.ShapeDtypeStruct(load.shape, F32),
        compiler_params=pltpu.CompilerParams(vmem_limit_bytes=16 << 20),
    )(hit, load, rows, cols, tap_current.T)

    def vm(*shape):
        return pltpu.VMEM(shape, F32)

    ext0 = (n_rows + 2, n_cols + 2 * MARGIN, LANES)
    tall = {h: (n_rows >> h) + 2 * HALO[h] + 2 for h in range(1, LEVELS)}
    levels = range(1, LEVELS)
    nn = n_dev
    scratch = [
        vm(n_rows, n_cols, LANES), vm(*ext0), vm(*ext0),
        vm(n_rows + 1, n_cols, LANES), vm(n_rows + 1, n_cols + MARGIN, LANES),
        vm(n_rows + 1, n_cols, LANES), vm(n_cols + MARGIN, n_rows),
        vm(3, 2 * REACH + 1, PACK_ROWS, LANES),
    ]
    scratch += [vm(tall[h], WIDTH[h], LANES) for h in levels]
    scratch += [vm(tall[h], WIDTH[h] + 2 * MARGIN, LANES) for h in levels] * 2
    scratch += [vm(tall[h], WIDTH[h], LANES) for h in levels]
    scratch += [vm(tall[h], WIDTH[h] + MARGIN, LANES) for h in levels]
    scratch += [vm(tall[h], WIDTH[h], LANES) for h in levels]
    scratch += [vm(2, 3, WIDTH[h] + MARGIN, LANES) for h in levels]
    scratch += [vm(n_dev, 32, LANES), vm(n_dev, 32, LANES), vm(n_dev + 8, 32 + 16, LANES), vm(12, 8, LANES)]
    scratch += [vm(nn >> l, 64, 32) for l in range(1, 6)]
    scratch += [vm(nn >> l, 32, 64) for l in range(1, 6)]
    scratch += [vm(nn >> l, 64, 32) for l in range(1, 6)]
    scratch += [vm(nn >> l, 32, 32) for l in range(1, 6)] + [vm(1, 32, 32)]
    scratch += [
        pltpu.SemaphoreType.DMA((N_COPIES,)),
        pltpu.SemaphoreType.DMA((N_COPIES,)),
        pltpu.SemaphoreType.DMA((1,)),
    ]
    return pl.pallas_call(
        functools.partial(cycle_kernel, n_grp, n_dev, n_rows, n_cols),
        out_shape=jax.ShapeDtypeStruct(load.shape, F32),
        in_specs=[
            pl.BlockSpec(memory_space=pl.ANY),
            pl.BlockSpec(memory_space=pltpu.VMEM),
            pl.BlockSpec(memory_space=pltpu.VMEM),
            pl.BlockSpec(memory_space=pltpu.SMEM),
        ],
        out_specs=pl.BlockSpec(memory_space=pl.ANY),
        scratch_shapes=scratch,
        compiler_params=pltpu.CompilerParams(
            collective_id=0, has_side_effects=True, vmem_limit_bytes=63 << 20
        ),
    )(source, east_class, north_class, cond_table)


def solution(mesh):
    return jax.shard_map(
        functools.partial(body, mesh.shape["grp"], mesh.shape["dev"]),
        mesh=mesh,
        in_specs=(P("grp", "dev", None), P("grp", "dev"), P("grp", "dev"), P(), P(), P()),
        out_specs=P("grp", "dev", None),
        check_vma=False,
    )
```

```python
import functools

import jax
import jax.numpy as jnp
from jax import lax
from jax.experimental import pallas as pl
from jax.experimental.pallas import tpu as pltpu
from jax.sharding import PartitionSpec as P

MESH = pl.DeviceIdType.MESH
HI = lax.Precision.HIGHEST
F32 = jnp.float32
LEVELS = 5
SHUNT = 0.01
RELAX = 0.8
LANES = 128

HALO = {1: 4, 2: 5, 3: 5, 4: 5}
WIDTH = {1: 24, 2: 24, 3: 16, 4: 16}
OFFSET = {1: 4, 2: 8, 3: 6, 4: 6}
PACK_E = {1: 0, 2: 32, 3: 48, 4: 56}
PACK_N = {1: 16, 2: 40, 3: 52, 4: 58}
PACK_ROWS = 64
MARGIN = 8
REACH = 3
TABLE_PART = 32


def dot(a, b, dims=((1,), (0,))):
    return lax.dot_general(a, b, (dims, ((), ())), precision=HI, preferred_element_type=F32)


def iota(shape, dim):
    return lax.broadcasted_iota(jnp.int32, shape, dim)


def rows_loop(lo, hi, fn, unroll=1):
    def step(i, carry):
        fn(i)
        return carry

    lax.fori_loop(lo, hi, step, 0, unroll=unroll)


def tap_kernel(n_rows, n_cols, shift, taps_ref, cur_ref, table_hbm, slot_ref, table, sems):
    far = 1 << 24
    taps = taps_ref[...]
    cur = cur_ref[...]
    rows = jnp.right_shift(taps, shift) - lax.axis_index("grp") * n_rows
    cols = jnp.bitwise_and(taps, (1 << shift) - 1) - lax.axis_index("dev") * n_cols
    inside = (rows >= 0) & (rows < n_rows) & (cols >= 0) & (cols < n_cols)
    rows = jnp.where(inside, rows, far)
    col_ids = iota((n_cols, LANES), 0)

    def clear(i, carry):
        slot_ref[i] = 0
        return carry

    lax.fori_loop(0, n_rows, clear, 0, unroll=8)
    table[0] = jnp.zeros((n_cols, LANES), F32)

    def more(carry):
        return carry[1] < far

    def one(carry):
        used, row = carry
        following = jnp.min(jnp.where(rows > row, rows, far))
        here = jnp.where(rows == row, cur, 0.0)
        total = jnp.zeros((n_cols, LANES), F32)
        for k in range(taps.shape[0]):
            total += jnp.where(cols[k : k + 1] == col_ids, here[k : k + 1], 0.0)
        table[used] = total
        slot_ref[row] = used
        return used + 1, following

    used, _ = lax.while_loop(more, one, (jnp.int32(1), jnp.min(rows)))

    def part(c):
        at = pl.ds(c * TABLE_PART, TABLE_PART)
        return pltpu.make_async_copy(table.at[at], table_hbm.at[at], sems.at[c])

    for c in range(table.shape[0] // TABLE_PART):

        @pl.when(used > c * TABLE_PART)
        def _():
            part(c).start()

    for c in range(table.shape[0] // TABLE_PART):

        @pl.when(used > c * TABLE_PART)
        def _():
            part(c).wait()


def around(dist):
    return [
        (di, dd)
        for di in (-1, 0, 1)
        for dd in range(-dist, dist + 1)
        if (di, dd) != (0, 0)
    ]


def overlap(step, size, halo):
    low = max(0, step * size - halo)
    high = min(size, step * size + size + halo)
    return low, high - low


def cycle_kernel(
    n_grp, n_dev, n_rows, n_cols,
    load_hbm, table_hbm, slot_ref, east_ref, north_ref, tab_ref,
    out_hbm,
    s0, u0, v0, e0, n0, w0, nt_ext, pack,
    s1, s2, s3, s4, u1, u2, u3, u4, v1, v2, v3, v4,
    e1, e2, e3, e4, n1, n2, n3, n4, w1, w2, w3, w4,
    cx1, cx2, cx3, cx4,
    g_cond, g_src, x_ext, c5,
    m1, m2, m3, m4, m5, y1, y2, y3, y4, y5, t1, t2, t3, t4, t5, p1, p2, p3, p4, p5, p6,
    send, recv, local,
):
    g = lax.axis_index("grp")
    d = lax.axis_index("dev")
    S = {1: s1, 2: s2, 3: s3, 4: s4}
    U = {0: u0, 1: u1, 2: u2, 3: u3, 4: u4}
    V = {0: v0, 1: v1, 2: v2, 3: v3, 4: v4}
    E = {0: e0, 1: e1, 2: e2, 3: e3, 4: e4}
    N = {0: n0, 1: n1, 2: n2, 3: n3, 4: n4}
    W = {0: w0, 1: w1, 2: w2, 3: w3, 4: w4}
    CX = {1: cx1, 2: cx2, 3: cx3, 4: cx4}
    S[0] = s0
    MT = {1: m1, 2: m2, 3: m3, 4: m4, 5: m5}
    YY = {1: y1, 2: y2, 3: y3, 4: y4, 5: y5}
    YT = {1: t1, 2: t2, 3: t3, 4: t4, 5: t5}
    PP = {1: p1, 2: p2, 3: p3, 4: p4, 5: p5, 6: p6}
    R = {h: n_rows >> h for h in range(6)}
    C = {h: n_cols >> h for h in range(6)}
    H = dict(HALO)
    H[0] = 0
    JP = dict(WIDTH)
    JP[0] = n_cols
    OJ = dict(OFFSET)
    OJ[0] = 0

    counter = [0]

    def take():
        counter[0] += 1
        return counter[0] - 1

    def at(di, dd):
        return (lax.rem(g + (di + n_grp), n_grp), lax.rem(d + (dd + n_dev), n_dev))

    def remote(src, dst, device):
        m = take()
        return pltpu.make_async_remote_copy(
            src_ref=src, dst_ref=dst, send_sem=send.at[m], recv_sem=recv.at[m],
            device_id=device, device_id_type=MESH,
        )

    zd = lax.rem(d, 8)
    yd = d // 8
    near = [(o, (g, yd * 8 + lax.rem(zd + o, 8))) for o in range(1, 8)]
    far = [
        (lax.rem(g + a, n_grp), lax.rem(yd + b, 4) * 8 + zd)
        for a in range(n_grp)
        for b in range(4)
        if (a, b) != (0, 0)
    ]
    partners = [at(di, dd) for di, dd in around(REACH)] + [dev for _, dev in near] + far

    barrier = pltpu.get_barrier_semaphore()
    for dev in partners:
        pl.semaphore_signal(barrier, inc=1, device_id=dev, device_id_type=MESH)

    own_rows = pl.ds(0, n_rows)
    fetch = pltpu.make_async_copy(load_hbm, s0, local.at[0])
    fetch.start()
    fetch_table = pltpu.make_async_copy(
        table_hbm.at[pl.ds(0, n_rows + 1)],
        v0.at[pl.ds(0, n_rows + 1), pl.ds(MARGIN, n_cols), :],
        local.at[1],
    )
    fetch_table.start()

    def conductance(cls):
        value = jnp.full(cls.shape, tab_ref[0], F32)
        for c in range(1, 8):
            value = jnp.where(cls == c, tab_ref[c], value)
        return value

    rows_c = iota((n_cols, n_rows), 1)
    cols_c = iota((n_cols, n_rows), 0)
    et = conductance(east_ref[...])
    et = jnp.where((rows_c == n_rows - 1) & (g == n_grp - 1), 0.0, et)
    nt = conductance(north_ref[...])
    nt = jnp.where((cols_c == n_cols - 1) & (d == n_dev - 1), 0.0, nt)
    nt_ext[pl.ds(MARGIN, n_cols), :] = nt

    packed = jnp.zeros((PACK_ROWS, LANES), F32)
    ri = iota((n_rows, LANES), 0)
    li = iota((n_rows, LANES), 1)
    pr = iota((PACK_ROWS, n_cols), 0)
    pj = iota((PACK_ROWS, n_cols), 1)
    for h in range(1, LEVELS):
        f = 1 << h
        last = jnp.where(ri == li * f + (f - 1), 1.0, 0.0)
        every = jnp.where(ri // f == li, 1.0, 0.0)
        qe = dot(et, last)
        qn = dot(nt, every)
        re, rn = pr - PACK_E[h], pr - PACK_N[h]
        pick_e = jnp.where((re >= 0) & (re < C[h]) & (pj // f == re), 1.0, 0.0)
        pick_n = jnp.where((rn >= 0) & (rn < C[h]) & (pj == rn * f + (f - 1)), 1.0, 0.0)
        packed += dot(pick_e, qe) + dot(pick_n, qn)
    pack[1, REACH] = packed

    si = iota((R[5], n_rows), 0)
    ci = iota((R[5], n_rows), 1)
    fe = jnp.where(ci == si * 32 + 31, 1.0, 0.0)
    fn_ = jnp.where(ci // 32 == si, 1.0, 0.0)
    e5 = jnp.sum(dot(fe, et, ((1,), (1,))), axis=1, keepdims=True)
    n5s = dot(fn_, nt, ((1,), (1,)))
    n5 = jnp.sum(jnp.where(iota(n5s.shape, 1) == n_cols - 1, n5s, 0.0), axis=1, keepdims=True)
    both = jnp.where(iota((R[5], LANES), 1) < 64, e5, n5)
    mine8 = pl.ds(pl.multiple_of(g * 8, 8), 8)
    g_cond[d, mine8, :] = both

    pl.semaphore_wait(barrier, len(partners))

    def gather_near(buf):
        return [
            remote(buf.at[d, mine8, :], buf.at[d, mine8, :], dev) for _, dev in near
        ]

    def gather_far(buf):
        slab = pl.ds(pl.multiple_of(yd * 8, 8), 8)
        return [remote(buf.at[slab, mine8, :], buf.at[slab, mine8, :], dev) for dev in far]

    def start(copies):
        for c in copies:
            c.start()

    def wait(copies):
        for c in copies:
            c.wait()

    north_edge = [
        remote(nt_ext.at[pl.ds(MARGIN + n_cols - 1, 1), :], nt_ext.at[pl.ds(MARGIN - 1, 1), :], at(0, 1))
    ]
    start(north_edge)
    cond_near = gather_near(g_cond)
    start(cond_near)
    pack_copies = []
    for di, dd in around(REACH):
        lo = {0: 0, 1: 0, 2: 48, 3: 56}[abs(dd)]
        part = pl.ds(lo, PACK_ROWS - lo)
        pack_copies.append(
            remote(pack.at[1, REACH, part, :], pack.at[1 - di, REACH - dd, part, :], at(di, dd))
        )
    start(pack_copies)

    def spread(block, lane, width):
        ids = iota(block.shape, 1)
        col = jnp.sum(jnp.where(ids == lane, block, 0.0), axis=1, keepdims=True)
        return jnp.broadcast_to(col, (width, LANES))

    for half in range(n_rows // LANES):
        blk = et[:, half * LANES : (half + 1) * LANES]

        def fill(i, blk=blk, half=half):
            e0[half * LANES + i + 1] = spread(blk, i, n_cols)

        rows_loop(0, LANES, fill, unroll=4)
    east_edge = [remote(e0.at[n_rows], e0.at[0], at(1, 0))]
    start(east_edge)
    wait(north_edge)
    for half in range(n_rows // LANES):
        blk = nt_ext[:, half * LANES : (half + 1) * LANES]

        def fill(i, blk=blk, half=half):
            n0[half * LANES + i + 1] = spread(blk, i, n_cols + MARGIN)

        rows_loop(0, LANES, fill, unroll=4)

    wait(cond_near)
    cond_far = gather_far(g_cond)
    start(cond_far)
    wait(east_edge)

    def win(h, shift=0):
        return pl.ds(MARGIN + shift, JP[h])

    def diagonal(h, r, shunt):
        return shunt + E[h][r] + E[h][r - 1] + N[h][r, win(h), :] + N[h][r, win(h, -1), :]

    def around_sum(h, ref, r):
        return (
            E[h][r] * ref[r + 1, win(h), :]
            + E[h][r - 1] * ref[r - 1, win(h), :]
            + N[h][r, win(h), :] * ref[r, win(h, 1), :]
            + N[h][r, win(h, -1), :] * ref[r, win(h, -1), :]
        )

    def set_weights(h):
        shunt = SHUNT * 4.0**h

        def fill(r):
            W[h][r] = RELAX / diagonal(h, r, shunt)

        rows_loop(1, R[h] + 2 * H[h] + 1, fill, unroll=2)

    def s_row(h, r):
        return s0[r - 1] if h == 0 else S[h][r]

    def first(h):
        def fill(r):
            if h == 0:
                s0[r - 1] = v0[slot_ref[r - 1], win(0), :] - s0[r - 1]
            U[h][r, win(h), :] = W[h][r] * s_row(h, r)

        rows_loop(1, R[h] + 2 * H[h] + 1, fill, unroll=2)

    def presmooth(h):
        lo = 1 if h == 0 else 2

        def fill(r):
            V[h][r, win(h), :] = W[h][r] * (1.2 * s_row(h, r) + around_sum(h, U[h], r))

        rows_loop(lo, R[h] + 2 * H[h] + 2 - lo, fill, unroll=2)

    def restrict(h):
        shunt = SHUNT * 4.0**h

        def residual(r):
            return (
                s_row(h, r)
                + around_sum(h, V[h], r)
                - diagonal(h, r, shunt) * V[h][r, win(h), :]
            )

        base = H[h] + 1

        def fill(q):
            U[h][q, win(h), :] = residual(base + 2 * q) + residual(base + 2 * q + 1)

        rows_loop(0, R[h + 1], fill, unroll=2)
        cc = C[h + 1]

        def halve(q):
            a = U[h][q, pl.ds(MARGIN + OJ[h], cc, stride=2), :]
            b = U[h][q, pl.ds(MARGIN + OJ[h] + 1, cc, stride=2), :]
            if h == LEVELS - 1:
                g_src[d, pl.ds(g * 8 + q, 1), :] = a + b
            else:
                S[h + 1][q + H[h + 1] + 1, pl.ds(OJ[h + 1], cc), :] = a + b

        rows_loop(0, R[h + 1], halve, unroll=2)

    def edges(ref):
        rows = pl.ds(1, n_rows)
        cols = pl.ds(MARGIN, n_cols)
        return [
            remote(ref.at[rows, pl.ds(MARGIN + n_cols - 1, 1), :], ref.at[rows, pl.ds(MARGIN - 1, 1), :], at(0, 1)),
            remote(ref.at[rows, pl.ds(MARGIN, 1), :], ref.at[rows, pl.ds(MARGIN + n_cols, 1), :], at(0, -1)),
            remote(ref.at[n_rows, cols, :], ref.at[0, cols, :], at(1, 0)),
            remote(ref.at[1, cols, :], ref.at[n_rows + 1, cols, :], at(-1, 0)),
        ]

    def halos(h):
        dist = -(-H[h] // C[h])
        copies = []
        for di, dd in around(dist):
            i0, ni = overlap(di, R[h], H[h])
            j0, nj = overlap(dd, C[h], H[h])
            src = S[h].at[pl.ds(i0 + H[h] + 1, ni), pl.ds(j0 + OJ[h], nj), :]
            dst = S[h].at[
                pl.ds(i0 - di * R[h] + H[h] + 1, ni), pl.ds(j0 - dd * C[h] + OJ[h], nj), :
            ]
            copies.append(remote(src, dst, at(di, dd)))
        return copies

    set_weights(0)
    fetch.wait()
    fetch_table.wait()
    first(0)
    u_edges = edges(u0)
    start(u_edges)

    def spread_level(h):
        width = MARGIN + JP[h]
        for t, base in ((0, PACK_E[h]), (1, PACK_N[h])):
            for di in range(3):
                for dd in range(-REACH, REACH + 1):
                    first_j = dd * C[h] + OJ[h] + MARGIN
                    lo = max(first_j, MARGIN - 1)
                    hi = min(first_j + C[h], width)
                    if hi > lo and abs(dd) <= -(-(H[h] + 1) // C[h]):
                        CX[h][t, di, pl.ds(lo, hi - lo), :] = pack[
                            di, dd + REACH, pl.ds(base + lo - first_j, hi - lo), :
                        ]

        def fill(i, di, shift):
            r = i + H[h] + 1 + shift
            E[h][r] = spread(CX[h][0, di, pl.ds(MARGIN, JP[h]), :], i, JP[h])
            N[h][r] = spread(CX[h][1, di], i, width)

        rows_loop(R[h] - H[h] - 1, R[h], functools.partial(fill, di=0, shift=-R[h]))
        rows_loop(0, R[h], functools.partial(fill, di=1, shift=0), unroll=4)
        rows_loop(0, H[h] + 1, functools.partial(fill, di=2, shift=R[h]))
        set_weights(h)

    nb = n_dev
    nn = n_grp * R[5]
    sub = iota((nn, nn), 0)
    lane = iota((nn, nn), 1)
    eye = sub == lane
    shunt5 = SHUNT * 4.0**LEVELS

    def coarse_block(k):
        both = g_cond[k]
        ee = both[:, :nn]
        low = pltpu.roll(both, 1, 0)[:, :nn]
        nc = pltpu.roll(both, 64, 1)[:, :nn]
        before = pltpu.roll(g_cond[(k - 1) % nb], 64, 1)[:, :nn]
        block = jnp.where(eye, shunt5 + ee + low + nc + before, 0.0)
        block = jnp.where(lane == sub + 1, -ee, block)
        block = jnp.where(lane == sub - 1, -low, block)
        return block, jnp.where(eye, -nc, 0.0), jnp.where(eye, -before, 0.0)

    def invert(ref):
        count = ref.shape[0]
        l3 = iota((count, nn, nn), 2)
        s3_ = iota((count, nn, nn), 1)
        lr = iota((count, 1, nn), 2)

        def step(k, carry):
            mat = ref[...]
            row = ref[:, pl.ds(k, 1), :]
            pivot = 1.0 / jnp.sum(jnp.where(lr == k, row, 0.0), axis=2, keepdims=True)
            col = jnp.sum(jnp.where(l3 == k, mat, 0.0), axis=2, keepdims=True)
            col = jnp.where(s3_ == k, -1.0, col)
            row = jnp.where(lr == k, pivot, row * pivot)
            ref[...] = jnp.where((l3 == k) | (s3_ == k), 0.0, mat) - col * row
            return carry

        lax.fori_loop(0, nn, step, 0)

    even = {}

    def matrices():
        even[1] = []
        for q in range(nb // 2):
            even[1].append(coarse_block(2 * q)[0])
            block, right, left = coarse_block(2 * q + 1)
            PP[1][q] = block
            MT[1][q] = jnp.concatenate([right, left], axis=0)

    def eliminate(lev):
        half = nb >> lev
        invert(PP[lev])
        zs = []
        for q in range(half):
            mt = MT[lev][q]
            inv = PP[lev][q]
            yt = dot(mt, inv)
            YT[lev][q] = yt
            YY[lev][q] = dot(inv, mt, ((1,), (1,)))
            zs.append(dot(yt, mt, ((1,), (1,))))
        new = []
        for q in range(half):
            block = even[lev][q] - zs[q][nn:, nn:]
            if q > 0:
                block = block - zs[q - 1][:nn, :nn]
            new.append(block)
        if lev == 5:
            PP[6][0] = new[0]
        else:
            for q in range(half // 2):
                odd = 2 * q + 1
                PP[lev + 1][q] = new[odd]
                MT[lev + 1][q] = jnp.concatenate(
                    [-zs[odd][:nn, nn:], -zs[odd - 1][nn:, :nn]], axis=0
                )
            even[lev + 1] = new[0::2]

    wait(pack_copies)
    spread_level(1)
    wait(u_edges)
    presmooth(0)
    v_edges = edges(v0)
    start(v_edges)
    for h in range(2, LEVELS):
        spread_level(h)
    wait(cond_far)
    matrices()
    wait(v_edges)
    restrict(0)
    for h in range(1, LEVELS):
        copies = halos(h)
        start(copies)
        eliminate(h)
        wait(copies)
        first(h)
        presmooth(h)
        restrict(h)
    src_near = gather_near(g_src)
    start(src_near)
    eliminate(5)
    wait(src_near)
    src_far = gather_far(g_src)
    start(src_far)
    invert(PP[6])
    x_ext[...] = jnp.zeros_like(x_ext)
    wait(src_far)

    for lev in range(1, 6):
        st = 1 << (lev - 1)
        for q in range(nb >> lev):
            odd = (2 * q + 1) * st
            upd = dot(YT[lev][q], g_src[odd])
            g_src[odd - st] = g_src[odd - st] - upd[nn:]
            if odd + st < nb:
                g_src[odd + st] = g_src[odd + st] - upd[:nn]
    inner = pl.ds(MARGIN, nn)
    x_ext[4, inner, :] = dot(PP[6][0], g_src[0])
    for lev in range(5, 0, -1):
        st = 1 << (lev - 1)
        for q in range(nb >> lev):
            odd = (2 * q + 1) * st
            x = dot(PP[lev][q], g_src[odd])
            y = YY[lev][q]
            x = x - dot(y[:, nn:], x_ext[4 + odd - st, inner, :])
            if odd + st < nb:
                x = x - dot(y[:, :nn], x_ext[4 + odd + st, inner, :])
            x_ext[4 + odd, inner, :] = x

    for k in range(8):
        part = x_ext[d + 1 + k, pl.ds(pl.multiple_of(g * 8, 8), 24), :]
        for i in range(12):
            c5[i, k : k + 1, :] = part[6 + i : 7 + i]

    def smooth(h, dst, ref, halo):
        lo = H[h] + 1 - halo if h else 1
        hi = R[h] + H[h] + 1 + halo if h else n_rows + 1

        def fill(r):
            dst[r, win(h), :] = 0.2 * ref[r, win(h), :] + W[h][r] * (
                s_row(h, r) + around_sum(h, ref, r)
            )

        rows_loop(lo, hi, fill, unroll=2)

    for h in range(LEVELS - 1, 0, -1):
        p = H[h] - 1
        first_q = -(-p // 2)
        size = JP[h] // 2

        def lift(q, h=h, size=size):
            if h == LEVELS - 1:
                coarse = c5[q + 2]
            else:
                cofs = MARGIN + OJ[h + 1] - OJ[h] // 2
                coarse = V[h + 1][q + H[h + 1] + 1, pl.ds(cofs, size), :]
            for a in range(2):
                r = 2 * q + a + H[h] + 1
                for b in range(2):
                    cols = pl.ds(MARGIN + b, size, stride=2)
                    V[h][r, cols, :] = V[h][r, cols, :] + coarse

        rows_loop(-first_q, R[h] // 2 + first_q, lift, unroll=2)
        smooth(h, U[h], V[h], p - 1)
        smooth(h, V[h], U[h], p - 2)

    half_cols = n_cols // 2

    def lift0(q, rows):
        coarse = V[1][q + H[1] + 1, pl.ds(MARGIN + OJ[1] - 1, half_cols + 2), :]
        for a in rows:
            r = 2 * q + a + 1
            for b in range(2):
                cols = pl.ds(MARGIN - 2 + b, half_cols + 2, stride=2)
                v0[r, cols, :] = v0[r, cols, :] + coarse

    lift0(-1, (1,))
    rows_loop(0, n_rows // 2, functools.partial(lift0, rows=(0, 1)), unroll=2)
    lift0(n_rows // 2, (0,))
    size = n_rows // PARTS
    order = [PARTS - 1] + list(range(PARTS - 1))
    flights = []
    cols = pl.ds(MARGIN, n_cols)
    for c in order:
        lo = 1 + c * size

        def fill(r):
            u0[r, win(0), :] = 0.2 * v0[r, win(0), :] + W[0][r] * (
                s0[r - 1] + around_sum(0, v0, r)
            )

        rows_loop(lo, lo + size, fill, unroll=2)
        rows = pl.ds(lo, size)
        mine = [
            remote(u0.at[rows, pl.ds(MARGIN + n_cols - 1, 1), :], u0.at[rows, pl.ds(MARGIN - 1, 1), :], at(0, 1)),
            remote(u0.at[rows, pl.ds(MARGIN, 1), :], u0.at[rows, pl.ds(MARGIN + n_cols, 1), :], at(0, -1)),
        ]
        if c == PARTS - 1:
            last_row = remote(u0.at[n_rows, cols, :], u0.at[0, cols, :], at(1, 0))
            mine.append(last_row)
        if c == 0:
            first_row = remote(u0.at[1, cols, :], u0.at[n_rows + 1, cols, :], at(-1, 0))
            mine.append(first_row)
        start(mine)
        flights.append(mine[:2])
    done = []
    for c, mine in zip(order, flights):
        wait(mine)
        if c == PARTS - 1:
            first_row.wait()
        if c == 0:
            last_row.wait()

        def last(r):
            s0[r - 1] = 0.2 * u0[r, win(0), :] + W[0][r] * (
                s0[r - 1] + around_sum(0, u0, r)
            )

        rows_loop(1 + c * size, 1 + c * size + size, last, unroll=2)
        rows = pl.ds(c * size, size)
        done.append(pltpu.make_async_copy(s0.at[rows], out_hbm.at[rows], local.at[2 + c]))
        done[-1].start()
    wait(done)
    assert counter[0] <= N_COPIES, counter[0]


N_COPIES = 160
PARTS = 4


def body(n_grp, n_dev, load, east_class, north_class, cond_table, taps, tap_current):
    n_rows, n_cols, cands = load.shape
    slots = -(-(n_rows + 1) // TABLE_PART) * TABLE_PART
    total = n_dev * n_cols
    assert total & (total - 1) == 0
    table, slot = pl.pallas_call(
        functools.partial(tap_kernel, n_rows, n_cols, total.bit_length() - 1),
        in_specs=[pl.BlockSpec(memory_space=pltpu.VMEM)] * 2,
        out_specs=[
            pl.BlockSpec(memory_space=pl.ANY),
            pl.BlockSpec(memory_space=pltpu.SMEM),
        ],
        out_shape=[
            jax.ShapeDtypeStruct((slots, n_cols, cands), F32),
            jax.ShapeDtypeStruct((n_rows,), jnp.int32),
        ],
        scratch_shapes=[
            pltpu.VMEM((slots, n_cols, cands), F32),
            pltpu.SemaphoreType.DMA((slots // TABLE_PART,)),
        ],
        compiler_params=pltpu.CompilerParams(vmem_limit_bytes=60 << 20),
    )(taps.T, tap_current.T)

    def vm(*shape):
        return pltpu.VMEM(shape, F32)

    ext0 = (n_rows + 2, n_cols + 2 * MARGIN, LANES)
    tall = {h: (n_rows >> h) + 2 * HALO[h] + 2 for h in range(1, LEVELS)}
    levels = range(1, LEVELS)
    nn = n_dev
    scratch = [
        vm(n_rows, n_cols, LANES), vm(*ext0), vm(*ext0),
        vm(n_rows + 1, n_cols, LANES), vm(n_rows + 1, n_cols + MARGIN, LANES),
        vm(n_rows + 1, n_cols, LANES), vm(n_cols + MARGIN, n_rows),
        vm(3, 2 * REACH + 1, PACK_ROWS, LANES),
    ]
    scratch += [vm(tall[h], WIDTH[h], LANES) for h in levels]
    scratch += [vm(tall[h], WIDTH[h] + 2 * MARGIN, LANES) for h in levels] * 2
    scratch += [vm(tall[h], WIDTH[h], LANES) for h in levels]
    scratch += [vm(tall[h], WIDTH[h] + MARGIN, LANES) for h in levels]
    scratch += [vm(tall[h], WIDTH[h], LANES) for h in levels]
    scratch += [vm(2, 3, WIDTH[h] + MARGIN, LANES) for h in levels]
    scratch += [vm(n_dev, 32, LANES), vm(n_dev, 32, LANES), vm(n_dev + 8, 32 + 16, LANES), vm(12, 8, LANES)]
    scratch += [vm(nn >> l, 64, 32) for l in range(1, 6)]
    scratch += [vm(nn >> l, 32, 64) for l in range(1, 6)]
    scratch += [vm(nn >> l, 64, 32) for l in range(1, 6)]
    scratch += [vm(nn >> l, 32, 32) for l in range(1, 6)] + [vm(1, 32, 32)]
    scratch += [
        pltpu.SemaphoreType.DMA((N_COPIES,)),
        pltpu.SemaphoreType.DMA((N_COPIES,)),
        pltpu.SemaphoreType.DMA((2 + PARTS,)),
    ]
    return pl.pallas_call(
        functools.partial(cycle_kernel, n_grp, n_dev, n_rows, n_cols),
        out_shape=jax.ShapeDtypeStruct(load.shape, F32),
        in_specs=[
            pl.BlockSpec(memory_space=pl.ANY),
            pl.BlockSpec(memory_space=pl.ANY),
            pl.BlockSpec(memory_space=pltpu.SMEM),
            pl.BlockSpec(memory_space=pltpu.VMEM),
            pl.BlockSpec(memory_space=pltpu.VMEM),
            pl.BlockSpec(memory_space=pltpu.SMEM),
        ],
        out_specs=pl.BlockSpec(memory_space=pl.ANY),
        scratch_shapes=scratch,
        compiler_params=pltpu.CompilerParams(
            collective_id=0, has_side_effects=True, vmem_limit_bytes=63 << 20
        ),
    )(load, table, slot, east_class.T, north_class.T, cond_table)


def solution(mesh):
    return jax.shard_map(
        functools.partial(body, mesh.shape["grp"], mesh.shape["dev"]),
        mesh=mesh,
        in_specs=(P("grp", "dev", None), P("grp", "dev"), P("grp", "dev"), P(), P(), P()),
        out_specs=P("grp", "dev", None),
        check_vma=False,
    )
```

```python
import functools

import jax
import jax.numpy as jnp
from jax import lax
from jax.experimental import pallas as pl
from jax.experimental.pallas import tpu as pltpu
from jax.sharding import PartitionSpec as P

MESH = pl.DeviceIdType.MESH
HI = lax.Precision.HIGHEST
F32 = jnp.float32
LEVELS = 5
SHUNT = 0.01
RELAX = 0.8
LANES = 128

HALO = {1: 4, 2: 5, 3: 5, 4: 5}
WIDTH = {1: 24, 2: 24, 3: 16, 4: 16}
OFFSET = {1: 4, 2: 8, 3: 6, 4: 6}
PACK_E = {1: 0, 2: 32, 3: 48, 4: 56}
PACK_N = {1: 16, 2: 40, 3: 52, 4: 58}
PACK_ROWS = 64
MARGIN = 8
REACH = 3
TABLE_PART = 32


def dot(a, b, dims=((1,), (0,))):
    return lax.dot_general(a, b, (dims, ((), ())), precision=HI, preferred_element_type=F32)


def iota(shape, dim):
    return lax.broadcasted_iota(jnp.int32, shape, dim)


def rows_loop(lo, hi, fn, unroll=1):
    def step(i, carry):
        fn(i)
        return carry

    lax.fori_loop(lo, hi, step, 0, unroll=unroll)


def tap_kernel(n_rows, n_cols, shift, taps_ref, cur_ref, table_hbm, slot_ref, table, sems):
    far = 1 << 24
    taps = taps_ref[...]
    cur = cur_ref[...]
    rows = jnp.right_shift(taps, shift) - lax.axis_index("grp") * n_rows
    cols = jnp.bitwise_and(taps, (1 << shift) - 1) - lax.axis_index("dev") * n_cols
    inside = (rows >= 0) & (rows < n_rows) & (cols >= 0) & (cols < n_cols)
    rows = jnp.where(inside, rows, far)
    col_ids = iota((n_cols, LANES), 0)

    def clear(i, carry):
        slot_ref[i] = 0
        return carry

    lax.fori_loop(0, n_rows, clear, 0, unroll=8)
    table[0] = jnp.zeros((n_cols, LANES), F32)

    def more(carry):
        return carry[1] < far

    def one(carry):
        used, row = carry
        following = jnp.min(jnp.where(rows > row, rows, far))
        here = jnp.where(rows == row, cur, 0.0)
        total = jnp.zeros((n_cols, LANES), F32)
        for k in range(taps.shape[0]):
            total += jnp.where(cols[k : k + 1] == col_ids, here[k : k + 1], 0.0)
        table[used] = total
        slot_ref[row] = used
        return used + 1, following

    used, _ = lax.while_loop(more, one, (jnp.int32(1), jnp.min(rows)))

    def part(c):
        at = pl.ds(c * TABLE_PART, TABLE_PART)
        return pltpu.make_async_copy(table.at[at], table_hbm.at[at], sems.at[c])

    for c in range(table.shape[0] // TABLE_PART):

        @pl.when(used > c * TABLE_PART)
        def _():
            part(c).start()

    for c in range(table.shape[0] // TABLE_PART):

        @pl.when(used > c * TABLE_PART)
        def _():
            part(c).wait()


def around(dist):
    return [
        (di, dd)
        for di in (-1, 0, 1)
        for dd in range(-dist, dist + 1)
        if (di, dd) != (0, 0)
    ]


def overlap(step, size, halo):
    low = max(0, step * size - halo)
    high = min(size, step * size + size + halo)
    return low, high - low


def cycle_kernel(
    n_grp, n_dev, n_rows, n_cols,
    load_hbm, table_hbm, slot_ref, east_ref, north_ref, tab_ref,
    out_hbm,
    s0, u0, v0, e0, n0, w0, et_ref, nt_ext, pack,
    s1, s2, s3, s4, u1, u2, u3, u4, v1, v2, v3, v4,
    e1, e2, e3, e4, n1, n2, n3, n4, w1, w2, w3, w4,
    cx1, cx2, cx3, cx4,
    g_cond, g_src, x_ext, c5,
    m1, m2, m3, m4, m5, y1, y2, y3, y4, y5, t1, t2, t3, t4, t5, p1, p2, p3, p4, p5, p6,
    send, recv, local,
):
    g = lax.axis_index("grp")
    d = lax.axis_index("dev")
    S = {1: s1, 2: s2, 3: s3, 4: s4}
    U = {0: u0, 1: u1, 2: u2, 3: u3, 4: u4}
    V = {0: v0, 1: v1, 2: v2, 3: v3, 4: v4}
    E = {0: e0, 1: e1, 2: e2, 3: e3, 4: e4}
    N = {0: n0, 1: n1, 2: n2, 3: n3, 4: n4}
    W = {0: w0, 1: w1, 2: w2, 3: w3, 4: w4}
    CX = {1: cx1, 2: cx2, 3: cx3, 4: cx4}
    S[0] = s0
    MT = {1: m1, 2: m2, 3: m3, 4: m4, 5: m5}
    YY = {1: y1, 2: y2, 3: y3, 4: y4, 5: y5}
    YT = {1: t1, 2: t2, 3: t3, 4: t4, 5: t5}
    PP = {1: p1, 2: p2, 3: p3, 4: p4, 5: p5, 6: p6}
    R = {h: n_rows >> h for h in range(6)}
    C = {h: n_cols >> h for h in range(6)}
    H = dict(HALO)
    H[0] = 0
    JP = dict(WIDTH)
    JP[0] = n_cols
    OJ = dict(OFFSET)
    OJ[0] = 0

    counter = [0]

    def take():
        counter[0] += 1
        return counter[0] - 1

    def at(di, dd):
        return (lax.rem(g + (di + n_grp), n_grp), lax.rem(d + (dd + n_dev), n_dev))

    def remote(src, dst, device):
        m = take()
        return pltpu.make_async_remote_copy(
            src_ref=src, dst_ref=dst, send_sem=send.at[m], recv_sem=recv.at[m],
            device_id=device, device_id_type=MESH,
        )

    zd = lax.rem(d, 8)
    yd = d // 8
    near = [(o, (g, yd * 8 + lax.rem(zd + o, 8))) for o in range(1, 8)]
    far = [
        (lax.rem(g + a, n_grp), lax.rem(yd + b, 4) * 8 + zd)
        for a in range(n_grp)
        for b in range(4)
        if (a, b) != (0, 0)
    ]
    partners = [at(di, dd) for di, dd in around(REACH)] + [dev for _, dev in near] + far

    barrier = pltpu.get_barrier_semaphore()
    for dev in partners:
        pl.semaphore_signal(barrier, inc=1, device_id=dev, device_id_type=MESH)

    own_rows = pl.ds(0, n_rows)
    fetch = pltpu.make_async_copy(load_hbm, s0, local.at[0])
    fetch.start()
    fetch_table = pltpu.make_async_copy(
        table_hbm.at[pl.ds(0, n_rows + 1)],
        v0.at[pl.ds(0, n_rows + 1), pl.ds(MARGIN, n_cols), :],
        local.at[1],
    )
    fetch_table.start()

    def conductance(cls):
        value = jnp.full(cls.shape, tab_ref[0], F32)
        for c in range(1, 8):
            value = jnp.where(cls == c, tab_ref[c], value)
        return value

    rows_c = iota((n_cols, n_rows), 1)
    cols_c = iota((n_cols, n_rows), 0)
    et = conductance(east_ref[...])
    et = jnp.where((rows_c == n_rows - 1) & (g == n_grp - 1), 0.0, et)
    nt = conductance(north_ref[...])
    nt = jnp.where((cols_c == n_cols - 1) & (d == n_dev - 1), 0.0, nt)
    nt_ext[pl.ds(MARGIN, n_cols), :] = nt

    packed = jnp.zeros((PACK_ROWS, LANES), F32)
    ri = iota((n_rows, LANES), 0)
    li = iota((n_rows, LANES), 1)
    pr = iota((PACK_ROWS, n_cols), 0)
    pj = iota((PACK_ROWS, n_cols), 1)
    for h in range(1, LEVELS):
        f = 1 << h
        last = jnp.where(ri == li * f + (f - 1), 1.0, 0.0)
        every = jnp.where(ri // f == li, 1.0, 0.0)
        qe = dot(et, last)
        qn = dot(nt, every)
        re, rn = pr - PACK_E[h], pr - PACK_N[h]
        pick_e = jnp.where((re >= 0) & (re < C[h]) & (pj // f == re), 1.0, 0.0)
        pick_n = jnp.where((rn >= 0) & (rn < C[h]) & (pj == rn * f + (f - 1)), 1.0, 0.0)
        packed += dot(pick_e, qe) + dot(pick_n, qn)
    pack[1, REACH] = packed

    si = iota((R[5], n_rows), 0)
    ci = iota((R[5], n_rows), 1)
    fe = jnp.where(ci == si * 32 + 31, 1.0, 0.0)
    fn_ = jnp.where(ci // 32 == si, 1.0, 0.0)
    e5 = jnp.sum(dot(fe, et, ((1,), (1,))), axis=1, keepdims=True)
    n5s = dot(fn_, nt, ((1,), (1,)))
    n5 = jnp.sum(jnp.where(iota(n5s.shape, 1) == n_cols - 1, n5s, 0.0), axis=1, keepdims=True)
    both = jnp.where(iota((R[5], LANES), 1) < 64, e5, n5)
    mine8 = pl.ds(pl.multiple_of(g * 8, 8), 8)
    g_cond[d, mine8, :] = both

    pl.semaphore_wait(barrier, len(partners))

    def gather_near(buf):
        return [
            remote(buf.at[d, mine8, :], buf.at[d, mine8, :], dev) for _, dev in near
        ]

    def gather_far(buf):
        slab = pl.ds(pl.multiple_of(yd * 8, 8), 8)
        return [remote(buf.at[slab, mine8, :], buf.at[slab, mine8, :], dev) for dev in far]

    def start(copies):
        for c in copies:
            c.start()

    def wait(copies):
        for c in copies:
            c.wait()

    north_edge = [
        remote(nt_ext.at[pl.ds(MARGIN + n_cols - 1, 1), :], nt_ext.at[pl.ds(MARGIN - 1, 1), :], at(0, 1))
    ]
    start(north_edge)
    cond_near = gather_near(g_cond)
    start(cond_near)
    pack_copies = []
    for di, dd in around(REACH):
        lo = {0: 0, 1: 0, 2: 48, 3: 56}[abs(dd)]
        part = pl.ds(lo, PACK_ROWS - lo)
        pack_copies.append(
            remote(pack.at[1, REACH, part, :], pack.at[1 - di, REACH - dd, part, :], at(di, dd))
        )
    start(pack_copies)

    def spread(block, lane, width):
        return jnp.broadcast_to(block[:, lane : lane + 1], (width, LANES))

    et_ref[...] = et

    def spread_part(dst, src, width):
        def fill(half):
            base = pl.multiple_of(half * LANES, LANES)
            blk = src[:, pl.ds(base, LANES)]
            for i in range(LANES):
                dst[base + i + 1] = spread(blk, i, width)

        rows_loop(0, n_rows // LANES, fill)

    spread_part(e0, et_ref, n_cols)
    east_edge = [remote(e0.at[n_rows], e0.at[0], at(1, 0))]
    start(east_edge)
    wait(north_edge)
    spread_part(n0, nt_ext, n_cols + MARGIN)

    wait(cond_near)
    cond_far = gather_far(g_cond)
    start(cond_far)
    wait(east_edge)

    def win(h, shift=0):
        return pl.ds(MARGIN + shift, JP[h])

    def diagonal(h, r, shunt):
        return shunt + E[h][r] + E[h][r - 1] + N[h][r, win(h), :] + N[h][r, win(h, -1), :]

    def stencil(h, ref, lo, hi, emit, block=8):
        def some(r0, count):
            stencil_rows(h, ref, r0, count, emit)

        full = (hi - lo) // block
        rows_loop(0, full, lambda q: some(lo + q * block, block))
        if lo + full * block < hi:
            some(lo + full * block, hi - lo - full * block)

    def stencil_rows(h, ref, r0, count, emit):
        for t in range(JP[h] // 8):
            here = pl.ds(8 * t, 8)
            mid = pl.ds(MARGIN + 8 * t, 8)
            up = pl.ds(MARGIN + 8 * t + 1, 8)
            down = pl.ds(MARGIN + 8 * t - 1, 8)
            below = ref[r0 - 1, mid, :]
            centre = ref[r0, mid, :]
            low = E[h][r0 - 1, here, :]
            for a in range(count):
                r = r0 + a
                above = ref[r + 1, mid, :]
                high = E[h][r, here, :]
                right = N[h][r, mid, :]
                left = N[h][r, down, :]
                near = (
                    high * above
                    + low * below
                    + right * ref[r, up, :]
                    + left * ref[r, down, :]
                )
                emit(r, t, centre, near, high + low + right + left)
                below, centre, low = centre, above, high

    def set_weights(h):
        shunt = SHUNT * 4.0**h

        def fill(r):
            W[h][r] = RELAX / diagonal(h, r, shunt)

        rows_loop(1, R[h] + 2 * H[h] + 1, fill, unroll=2)

    def s_row(h, r):
        return s0[r - 1] if h == 0 else S[h][r]

    def first(h):
        def fill(r):
            if h == 0:
                s0[r - 1] = v0[slot_ref[r - 1], win(0), :] - s0[r - 1]
            U[h][r, win(h), :] = W[h][r] * s_row(h, r)

        rows_loop(1, R[h] + 2 * H[h] + 1, fill, unroll=2)

    def s_tile(h, r, t):
        here = pl.ds(8 * t, 8)
        return s0[r - 1, here, :] if h == 0 else S[h][r, here, :]

    def presmooth(h):
        lo = 1 if h == 0 else 2

        def emit(r, t, centre, near, total):
            V[h][r, pl.ds(MARGIN + 8 * t, 8), :] = W[h][r, pl.ds(8 * t, 8), :] * (
                1.2 * s_tile(h, r, t) + near
            )

        stencil(h, U[h], lo, R[h] + 2 * H[h] + 2 - lo, emit)

    def restrict(h):
        shunt = SHUNT * 4.0**h
        base = H[h] + 1
        block = min(8, R[h])

        def pairs(q):
            held = {}

            def emit(r, t, centre, near, total):
                value = s_tile(h, r, t) + near - (shunt + total) * centre
                if t in held:
                    first_r, first_value = held.pop(t)
                    U[h][first_r, pl.ds(MARGIN + 8 * t, 8), :] = first_value + value
                else:
                    held[t] = (q * (block // 2) + pairs_done[t], value)
                    pairs_done[t] += 1

            pairs_done = {t: 0 for t in range(JP[h] // 8)}
            stencil_rows(h, V[h], base + q * block, block, emit)

        rows_loop(0, R[h] // block, pairs)
        cc = C[h + 1]

        def halve(q):
            a = U[h][q, pl.ds(MARGIN + OJ[h], cc, stride=2), :]
            b = U[h][q, pl.ds(MARGIN + OJ[h] + 1, cc, stride=2), :]
            if h == LEVELS - 1:
                g_src[d, pl.ds(g * 8 + q, 1), :] = a + b
            else:
                S[h + 1][q + H[h + 1] + 1, pl.ds(OJ[h + 1], cc), :] = a + b

        rows_loop(0, R[h + 1], halve, unroll=2)

    def edges(ref):
        rows = pl.ds(1, n_rows)
        cols = pl.ds(MARGIN, n_cols)
        return [
            remote(ref.at[rows, pl.ds(MARGIN + n_cols - 1, 1), :], ref.at[rows, pl.ds(MARGIN - 1, 1), :], at(0, 1)),
            remote(ref.at[rows, pl.ds(MARGIN, 1), :], ref.at[rows, pl.ds(MARGIN + n_cols, 1), :], at(0, -1)),
            remote(ref.at[n_rows, cols, :], ref.at[0, cols, :], at(1, 0)),
            remote(ref.at[1, cols, :], ref.at[n_rows + 1, cols, :], at(-1, 0)),
        ]

    def halos(h):
        dist = -(-H[h] // C[h])
        copies = []
        for di, dd in around(dist):
            i0, ni = overlap(di, R[h], H[h])
            j0, nj = overlap(dd, C[h], H[h])
            src = S[h].at[pl.ds(i0 + H[h] + 1, ni), pl.ds(j0 + OJ[h], nj), :]
            dst = S[h].at[
                pl.ds(i0 - di * R[h] + H[h] + 1, ni), pl.ds(j0 - dd * C[h] + OJ[h], nj), :
            ]
            copies.append(remote(src, dst, at(di, dd)))
        return copies

    set_weights(0)
    fetch.wait()
    fetch_table.wait()
    first(0)
    u_edges = edges(u0)
    start(u_edges)

    def spread_level(h):
        width = MARGIN + JP[h]
        for t, base in ((0, PACK_E[h]), (1, PACK_N[h])):
            for di in range(3):
                for dd in range(-REACH, REACH + 1):
                    first_j = dd * C[h] + OJ[h] + MARGIN
                    lo = max(first_j, MARGIN - 1)
                    hi = min(first_j + C[h], width)
                    if hi > lo and abs(dd) <= -(-(H[h] + 1) // C[h]):
                        CX[h][t, di, pl.ds(lo, hi - lo), :] = pack[
                            di, dd + REACH, pl.ds(base + lo - first_j, hi - lo), :
                        ]

        for di, lo, hi in (
            (0, R[h] - H[h] - 1, R[h]),
            (1, 0, R[h]),
            (2, 0, H[h] + 1),
        ):
            east = CX[h][0, di, pl.ds(MARGIN, JP[h]), :]
            north = CX[h][1, di]
            for i in range(lo, hi):
                r = i + H[h] + 1 + (di - 1) * R[h]
                E[h][r] = spread(east, i, JP[h])
                N[h][r] = spread(north, i, width)

        set_weights(h)

    nb = n_dev
    nn = n_grp * R[5]
    sub = iota((nn, nn), 0)
    lane = iota((nn, nn), 1)
    eye = sub == lane
    shunt5 = SHUNT * 4.0**LEVELS

    def coarse_block(k):
        both = g_cond[k]
        ee = both[:, :nn]
        low = pltpu.roll(both, 1, 0)[:, :nn]
        nc = pltpu.roll(both, 64, 1)[:, :nn]
        before = pltpu.roll(g_cond[(k - 1) % nb], 64, 1)[:, :nn]
        block = jnp.where(eye, shunt5 + ee + low + nc + before, 0.0)
        block = jnp.where(lane == sub + 1, -ee, block)
        block = jnp.where(lane == sub - 1, -low, block)
        return block, jnp.where(eye, -nc, 0.0), jnp.where(eye, -before, 0.0)

    def invert(ref):
        count = ref.shape[0]
        l3 = iota((count, nn, nn), 2)
        s3_ = iota((count, nn, nn), 1)
        lr = iota((count, 1, nn), 2)

        def step(k, carry):
            mat = ref[...]
            row = ref[:, pl.ds(k, 1), :]
            pivot = 1.0 / jnp.sum(jnp.where(lr == k, row, 0.0), axis=2, keepdims=True)
            col = jnp.sum(jnp.where(l3 == k, mat, 0.0), axis=2, keepdims=True)
            col = jnp.where(s3_ == k, -1.0, col)
            row = jnp.where(lr == k, pivot, row * pivot)
            ref[...] = jnp.where((l3 == k) | (s3_ == k), 0.0, mat) - col * row
            return carry

        lax.fori_loop(0, nn, step, 0)

    even = {}

    def matrices():
        even[1] = []
        for q in range(nb // 2):
            even[1].append(coarse_block(2 * q)[0])
            block, right, left = coarse_block(2 * q + 1)
            PP[1][q] = block
            MT[1][q] = jnp.concatenate([right, left], axis=0)

    def eliminate(lev):
        half = nb >> lev
        invert(PP[lev])
        zs = []
        for q in range(half):
            mt = MT[lev][q]
            inv = PP[lev][q]
            yt = dot(mt, inv)
            YT[lev][q] = yt
            YY[lev][q] = dot(inv, mt, ((1,), (1,)))
            zs.append(dot(yt, mt, ((1,), (1,))))
        new = []
        for q in range(half):
            block = even[lev][q] - zs[q][nn:, nn:]
            if q > 0:
                block = block - zs[q - 1][:nn, :nn]
            new.append(block)
        if lev == 5:
            PP[6][0] = new[0]
        else:
            for q in range(half // 2):
                odd = 2 * q + 1
                PP[lev + 1][q] = new[odd]
                MT[lev + 1][q] = jnp.concatenate(
                    [-zs[odd][:nn, nn:], -zs[odd - 1][nn:, :nn]], axis=0
                )
            even[lev + 1] = new[0::2]

    wait(pack_copies)
    spread_level(1)
    wait(u_edges)
    presmooth(0)
    v_edges = edges(v0)
    start(v_edges)
    for h in range(2, LEVELS):
        spread_level(h)
    wait(cond_far)
    matrices()
    wait(v_edges)
    restrict(0)
    for h in range(1, LEVELS):
        copies = halos(h)
        start(copies)
        eliminate(h)
        wait(copies)
        first(h)
        presmooth(h)
        restrict(h)
    src_near = gather_near(g_src)
    start(src_near)
    wait(src_near)
    src_far = gather_far(g_src)
    start(src_far)
    eliminate(5)
    invert(PP[6])
    x_ext[...] = jnp.zeros_like(x_ext)
    wait(src_far)

    for lev in range(1, 6):
        st = 1 << (lev - 1)
        for q in range(nb >> lev):
            odd = (2 * q + 1) * st
            upd = dot(YT[lev][q], g_src[odd])
            g_src[odd - st] = g_src[odd - st] - upd[nn:]
            if odd + st < nb:
                g_src[odd + st] = g_src[odd + st] - upd[:nn]
    inner = pl.ds(MARGIN, nn)
    x_ext[4, inner, :] = dot(PP[6][0], g_src[0])
    for lev in range(5, 0, -1):
        st = 1 << (lev - 1)
        for q in range(nb >> lev):
            odd = (2 * q + 1) * st
            x = dot(PP[lev][q], g_src[odd])
            y = YY[lev][q]
            x = x - dot(y[:, nn:], x_ext[4 + odd - st, inner, :])
            if odd + st < nb:
                x = x - dot(y[:, :nn], x_ext[4 + odd + st, inner, :])
            x_ext[4 + odd, inner, :] = x

    for k in range(8):
        part = x_ext[d + 1 + k, pl.ds(pl.multiple_of(g * 8, 8), 24), :]
        for i in range(12):
            c5[i, k : k + 1, :] = part[6 + i : 7 + i]

    def smooth(h, dst, ref, lo, hi):
        def emit(r, t, centre, near, total):
            dst[r, pl.ds(MARGIN + 8 * t, 8), :] = 0.2 * centre + W[h][r, pl.ds(8 * t, 8), :] * (
                s_tile(h, r, t) + near
            )

        stencil(h, ref, lo, hi, emit)

    for h in range(LEVELS - 1, 0, -1):
        p = H[h] - 1
        first_q = -(-p // 2)
        size = JP[h] // 2

        def lift(q, h=h, size=size):
            if h == LEVELS - 1:
                coarse = c5[q + 2]
            else:
                cofs = MARGIN + OJ[h + 1] - OJ[h] // 2
                coarse = V[h + 1][q + H[h + 1] + 1, pl.ds(cofs, size), :]
            for a in range(2):
                r = 2 * q + a + H[h] + 1
                for b in range(2):
                    cols = pl.ds(MARGIN + b, size, stride=2)
                    V[h][r, cols, :] = V[h][r, cols, :] + coarse

        rows_loop(-first_q, R[h] // 2 + first_q, lift, unroll=2)
        own = H[h] + 1
        smooth(h, U[h], V[h], own - (p - 1), own + R[h] + (p - 1))
        smooth(h, V[h], U[h], own - (p - 2), own + R[h] + (p - 2))

    half_cols = n_cols // 2

    def lift0(q, rows):
        coarse = V[1][q + H[1] + 1, pl.ds(MARGIN + OJ[1] - 1, half_cols + 2), :]
        for a in rows:
            r = 2 * q + a + 1
            for b in range(2):
                cols = pl.ds(MARGIN - 2 + b, half_cols + 2, stride=2)
                v0[r, cols, :] = v0[r, cols, :] + coarse

    lift0(-1, (1,))
    rows_loop(0, n_rows // 2, functools.partial(lift0, rows=(0, 1)), unroll=2)
    lift0(n_rows // 2, (0,))
    size = n_rows // PARTS
    order = [PARTS - 1] + list(range(PARTS - 1))
    flights = []
    cols = pl.ds(MARGIN, n_cols)
    for c in order:
        lo = 1 + c * size
        smooth(0, u0, v0, lo, lo + size)
        rows = pl.ds(lo, size)
        mine = [
            remote(u0.at[rows, pl.ds(MARGIN + n_cols - 1, 1), :], u0.at[rows, pl.ds(MARGIN - 1, 1), :], at(0, 1)),
            remote(u0.at[rows, pl.ds(MARGIN, 1), :], u0.at[rows, pl.ds(MARGIN + n_cols, 1), :], at(0, -1)),
        ]
        if c == PARTS - 1:
            last_row = remote(u0.at[n_rows, cols, :], u0.at[0, cols, :], at(1, 0))
            mine.append(last_row)
        if c == 0:
            first_row = remote(u0.at[1, cols, :], u0.at[n_rows + 1, cols, :], at(-1, 0))
            mine.append(first_row)
        start(mine)
        flights.append(mine[:2])
    done = []
    for c, mine in zip(order, flights):
        wait(mine)
        if c == PARTS - 1:
            first_row.wait()
        if c == 0:
            last_row.wait()

        def last(r, t, centre, near, total):
            here = pl.ds(8 * t, 8)
            s0[r - 1, here, :] = 0.2 * centre + w0[r, here, :] * (s0[r - 1, here, :] + near)

        stencil(0, u0, 1 + c * size, 1 + c * size + size, last)
        rows = pl.ds(c * size, size)
        done.append(pltpu.make_async_copy(s0.at[rows], out_hbm.at[rows], local.at[2 + c]))
        done[-1].start()
    wait(done)
    assert counter[0] <= N_COPIES, counter[0]


N_COPIES = 160
PARTS = 4


def body(n_grp, n_dev, load, east_class, north_class, cond_table, taps, tap_current):
    n_rows, n_cols, cands = load.shape
    slots = -(-(n_rows + 1) // TABLE_PART) * TABLE_PART
    total = n_dev * n_cols
    assert total & (total - 1) == 0
    table, slot = pl.pallas_call(
        functools.partial(tap_kernel, n_rows, n_cols, total.bit_length() - 1),
        in_specs=[pl.BlockSpec(memory_space=pltpu.VMEM)] * 2,
        out_specs=[
            pl.BlockSpec(memory_space=pl.ANY),
            pl.BlockSpec(memory_space=pltpu.SMEM),
        ],
        out_shape=[
            jax.ShapeDtypeStruct((slots, n_cols, cands), F32),
            jax.ShapeDtypeStruct((n_rows,), jnp.int32),
        ],
        scratch_shapes=[
            pltpu.VMEM((slots, n_cols, cands), F32),
            pltpu.SemaphoreType.DMA((slots // TABLE_PART,)),
        ],
        compiler_params=pltpu.CompilerParams(vmem_limit_bytes=60 << 20),
    )(taps.T, tap_current.T)

    def vm(*shape):
        return pltpu.VMEM(shape, F32)

    ext0 = (n_rows + 2, n_cols + 2 * MARGIN, LANES)
    tall = {h: (n_rows >> h) + 2 * HALO[h] + 2 for h in range(1, LEVELS)}
    levels = range(1, LEVELS)
    nn = n_dev
    scratch = [
        vm(n_rows, n_cols, LANES), vm(*ext0), vm(*ext0),
        vm(n_rows + 1, n_cols, LANES), vm(n_rows + 1, n_cols + MARGIN, LANES),
        vm(n_rows + 1, n_cols, LANES), vm(n_cols, n_rows), vm(n_cols + MARGIN, n_rows),
        vm(3, 2 * REACH + 1, PACK_ROWS, LANES),
    ]
    scratch += [vm(tall[h], WIDTH[h], LANES) for h in levels]
    scratch += [vm(tall[h], WIDTH[h] + 2 * MARGIN, LANES) for h in levels] * 2
    scratch += [vm(tall[h], WIDTH[h], LANES) for h in levels]
    scratch += [vm(tall[h], WIDTH[h] + MARGIN, LANES) for h in levels]
    scratch += [vm(tall[h], WIDTH[h], LANES) for h in levels]
    scratch += [vm(2, 3, WIDTH[h] + MARGIN, LANES) for h in levels]
    scratch += [vm(n_dev, 32, LANES), vm(n_dev, 32, LANES), vm(n_dev + 8, 32 + 16, LANES), vm(12, 8, LANES)]
    scratch += [vm(nn >> l, 64, 32) for l in range(1, 6)]
    scratch += [vm(nn >> l, 32, 64) for l in range(1, 6)]
    scratch += [vm(nn >> l, 64, 32) for l in range(1, 6)]
    scratch += [vm(nn >> l, 32, 32) for l in range(1, 6)] + [vm(1, 32, 32)]
    scratch += [
        pltpu.SemaphoreType.DMA((N_COPIES,)),
        pltpu.SemaphoreType.DMA((N_COPIES,)),
        pltpu.SemaphoreType.DMA((2 + PARTS,)),
    ]
    return pl.pallas_call(
        functools.partial(cycle_kernel, n_grp, n_dev, n_rows, n_cols),
        out_shape=jax.ShapeDtypeStruct(load.shape, F32),
        in_specs=[
            pl.BlockSpec(memory_space=pl.ANY),
            pl.BlockSpec(memory_space=pl.ANY),
            pl.BlockSpec(memory_space=pltpu.SMEM),
            pl.BlockSpec(memory_space=pltpu.VMEM),
            pl.BlockSpec(memory_space=pltpu.VMEM),
            pl.BlockSpec(memory_space=pltpu.SMEM),
        ],
        out_specs=pl.BlockSpec(memory_space=pl.ANY),
        scratch_shapes=scratch,
        compiler_params=pltpu.CompilerParams(
            collective_id=0, has_side_effects=True, vmem_limit_bytes=63 << 20
        ),
    )(load, table, slot, east_class.T, north_class.T, cond_table)


def solution(mesh):
    return jax.shard_map(
        functools.partial(body, mesh.shape["grp"], mesh.shape["dev"]),
        mesh=mesh,
        in_specs=(P("grp", "dev", None), P("grp", "dev"), P("grp", "dev"), P(), P(), P()),
        out_specs=P("grp", "dev", None),
        check_vma=False,
    )
```

```python
import functools

import jax
import jax.numpy as jnp
from jax import lax
from jax.experimental import pallas as pl
from jax.experimental.pallas import tpu as pltpu
from jax.sharding import PartitionSpec as P

MESH = pl.DeviceIdType.MESH
HI = lax.Precision.HIGHEST
F32 = jnp.float32
LEVELS = 5
SHUNT = 0.01
RELAX = 0.8
LANES = 128

HALO = {1: 6, 2: 5, 3: 6, 4: 5}
WIDTH = {1: 32, 2: 24, 3: 24, 4: 16}
OFFSET = {1: 7, 2: 8, 3: 7, 4: 6}
UPWARD = {1: 3, 2: 4, 3: 4, 4: 4}
DOWNWARD = {0: 0, 1: 6, 2: 2, 3: 6, 4: 2}
GROW = {0: 0, 1: 2, 2: 0, 3: 2, 4: 0}
PACK_E = {1: 0, 2: 32, 3: 48, 4: 56}
PACK_N = {1: 16, 2: 40, 3: 52, 4: 58}
PACK_ROWS = 64
MARGIN = 8
REACH = 3
TABLE_PART = 32


def dot(a, b, dims=((1,), (0,))):
    return lax.dot_general(a, b, (dims, ((), ())), precision=HI, preferred_element_type=F32)


def iota(shape, dim):
    return lax.broadcasted_iota(jnp.int32, shape, dim)


def rows_loop(lo, hi, fn, unroll=1):
    def step(i, carry):
        fn(i)
        return carry

    lax.fori_loop(lo, hi, step, 0, unroll=unroll)


def tap_kernel(n_rows, n_cols, shift, taps_ref, cur_ref, table_hbm, slot_ref, table, sems):
    far = 1 << 24
    taps = taps_ref[...]
    cur = cur_ref[...]
    rows = jnp.right_shift(taps, shift) - lax.axis_index("grp") * n_rows
    cols = jnp.bitwise_and(taps, (1 << shift) - 1) - lax.axis_index("dev") * n_cols
    inside = (rows >= 0) & (rows < n_rows) & (cols >= 0) & (cols < n_cols)
    rows = jnp.where(inside, rows, far)
    col_ids = iota((n_cols, LANES), 0)

    def clear(i, carry):
        slot_ref[i] = 0
        return carry

    lax.fori_loop(0, n_rows, clear, 0, unroll=8)
    table[0] = jnp.zeros((n_cols, LANES), F32)

    lower = jnp.where(inside, rows, -1)

    def more(carry):
        return carry[1] <= carry[2]

    def two(carry):
        used, low, high = carry
        after = jnp.min(jnp.where(rows > low, rows, far))
        before = jnp.max(jnp.where(lower < high, lower, -1))
        for step, row in enumerate((low, high)):
            here = jnp.where(rows == row, cur, 0.0)
            total = jnp.zeros((n_cols, LANES), F32)
            for k in range(taps.shape[0]):
                total += jnp.where(cols[k : k + 1] == col_ids, here[k : k + 1], 0.0)
            table[used + step] = total
            slot_ref[row] = used + step
        return used + 2, after, before

    used, _, _ = lax.while_loop(more, two, (jnp.int32(1), jnp.min(rows), jnp.max(lower)))

    def part(c):
        at = pl.ds(c * TABLE_PART, TABLE_PART)
        return pltpu.make_async_copy(table.at[at], table_hbm.at[at], sems.at[c])

    for c in range(table.shape[0] // TABLE_PART):

        @pl.when(used > c * TABLE_PART)
        def _():
            part(c).start()

    for c in range(table.shape[0] // TABLE_PART):

        @pl.when(used > c * TABLE_PART)
        def _():
            part(c).wait()


def around(dist):
    return [
        (di, dd)
        for di in (-1, 0, 1)
        for dd in range(-dist, dist + 1)
        if (di, dd) != (0, 0)
    ]


def overlap(step, size, halo):
    low = max(0, step * size - halo)
    high = min(size, step * size + size + halo)
    return low, high - low


def cycle_kernel(
    n_grp, n_dev, n_rows, n_cols,
    load_hbm, table_hbm, slot_ref, east_ref, north_ref, tab_ref,
    out_hbm,
    s0, u0, v0, e0, n0, w0, et_ref, nt_ext, pack,
    s1, s2, s3, s4, u1, u2, u3, u4, v1, v2, v3, v4,
    e1, e2, e3, e4, n1, n2, n3, n4, w1, w2, w3, w4,
    cx1, cx2, cx3, cx4, sx2, sx4,
    g_cond, g_src, x_ext, c5,
    m1, m2, m3, m4, m5, y1, y2, y3, y4, y5, t1, t2, t3, t4, t5, p1, p2, p3, p4, p5, p6,
    send, recv, local, own_sem,
):
    g = lax.axis_index("grp")
    d = lax.axis_index("dev")
    S = {1: s1, 2: s2, 3: s3, 4: s4}
    U = {0: u0, 1: u1, 2: u2, 3: u3, 4: u4}
    V = {0: v0, 1: v1, 2: v2, 3: v3, 4: v4}
    E = {0: e0, 1: e1, 2: e2, 3: e3, 4: e4}
    N = {0: n0, 1: n1, 2: n2, 3: n3, 4: n4}
    W = {0: w0, 1: w1, 2: w2, 3: w3, 4: w4}
    CX = {1: cx1, 2: cx2, 3: cx3, 4: cx4}
    S[0] = s0
    SX = {0: s0, 1: s1, 2: sx2, 3: s3, 4: sx4}
    BASE = {0: MARGIN, 1: 0, 2: 0, 3: 0, 4: 0}
    MT = {1: m1, 2: m2, 3: m3, 4: m4, 5: m5}
    YY = {1: y1, 2: y2, 3: y3, 4: y4, 5: y5}
    YT = {1: t1, 2: t2, 3: t3, 4: t4, 5: t5}
    PP = {1: p1, 2: p2, 3: p3, 4: p4, 5: p5, 6: p6}
    R = {h: n_rows >> h for h in range(6)}
    C = {h: n_cols >> h for h in range(6)}
    H = dict(HALO)
    H[0] = 0
    JP = dict(WIDTH)
    JP[0] = n_cols
    OJ = dict(OFFSET)
    OJ[0] = 0

    counter = [0]

    def take():
        counter[0] += 1
        return counter[0] - 1

    def at(di, dd):
        return (lax.rem(g + (di + n_grp), n_grp), lax.rem(d + (dd + n_dev), n_dev))

    def remote(src, dst, device):
        m = take()
        return pltpu.make_async_remote_copy(
            src_ref=src, dst_ref=dst, send_sem=send.at[m], recv_sem=recv.at[m],
            device_id=device, device_id_type=MESH,
        )

    zd = lax.rem(d, 8)
    yd = d // 8
    near = [(o, (g, yd * 8 + lax.rem(zd + o, 8))) for o in range(1, 8)]
    far = [
        (lax.rem(g + a, n_grp), lax.rem(yd + b, 4) * 8 + zd)
        for a in range(n_grp)
        for b in range(4)
        if (a, b) != (0, 0)
    ]
    partners = [at(di, dd) for di, dd in around(REACH)] + [dev for _, dev in near] + far

    barrier = pltpu.get_barrier_semaphore()
    for dev in partners:
        pl.semaphore_signal(barrier, inc=1, device_id=dev, device_id_type=MESH)

    own_rows = pl.ds(0, n_rows)
    fetch = pltpu.make_async_copy(load_hbm, s0, local.at[0])
    fetch.start()
    fetch_table = pltpu.make_async_copy(
        table_hbm.at[pl.ds(0, n_rows + 1)],
        v0.at[pl.ds(0, n_rows + 1), pl.ds(MARGIN, n_cols), :],
        local.at[1],
    )
    fetch_table.start()

    def conductance(cls):
        value = jnp.full(cls.shape, tab_ref[0], F32)
        for c in range(1, 8):
            value = jnp.where(cls == c, tab_ref[c], value)
        return value

    rows_c = iota((n_cols, n_rows), 1)
    cols_c = iota((n_cols, n_rows), 0)
    et = conductance(east_ref[...])
    et = jnp.where((rows_c == n_rows - 1) & (g == n_grp - 1), 0.0, et)
    nt = conductance(north_ref[...])
    nt = jnp.where((cols_c == n_cols - 1) & (d == n_dev - 1), 0.0, nt)
    nt_ext[pl.ds(MARGIN, n_cols), :] = nt

    packed = jnp.zeros((PACK_ROWS, LANES), F32)
    ri = iota((n_rows, LANES), 0)
    li = iota((n_rows, LANES), 1)
    pr = iota((PACK_ROWS, n_cols), 0)
    pj = iota((PACK_ROWS, n_cols), 1)
    for h in range(1, LEVELS):
        f = 1 << h
        last = jnp.where(ri == li * f + (f - 1), 1.0, 0.0)
        every = jnp.where(ri // f == li, 1.0, 0.0)
        qe = dot(et, last)
        qn = dot(nt, every)
        re, rn = pr - PACK_E[h], pr - PACK_N[h]
        pick_e = jnp.where((re >= 0) & (re < C[h]) & (pj // f == re), 1.0, 0.0)
        pick_n = jnp.where((rn >= 0) & (rn < C[h]) & (pj == rn * f + (f - 1)), 1.0, 0.0)
        packed += dot(pick_e, qe) + dot(pick_n, qn)
    pack[1, REACH] = packed

    si = iota((R[5], n_rows), 0)
    ci = iota((R[5], n_rows), 1)
    fe = jnp.where(ci == si * 32 + 31, 1.0, 0.0)
    fn_ = jnp.where(ci // 32 == si, 1.0, 0.0)
    e5 = jnp.sum(dot(fe, et, ((1,), (1,))), axis=1, keepdims=True)
    n5s = dot(fn_, nt, ((1,), (1,)))
    n5 = jnp.sum(jnp.where(iota(n5s.shape, 1) == n_cols - 1, n5s, 0.0), axis=1, keepdims=True)
    both = jnp.where(iota((R[5], LANES), 1) < 64, e5, n5)
    mine8 = pl.ds(pl.multiple_of(g * 8, 8), 8)
    g_cond[d, mine8, :] = both

    def spread(block, lane, width):
        return jnp.broadcast_to(block[:, lane : lane + 1], (width, LANES))

    et_ref[...] = et

    def spread_part(dst, src, first_row, width):
        def fill(half):
            base = pl.multiple_of(half * LANES, LANES)
            blk = src[first_row : first_row + width, pl.ds(base, LANES)]
            for i in range(LANES):
                dst[base + i + 1, pl.ds(first_row, width), :] = spread(blk, i, width)

        rows_loop(0, n_rows // LANES, fill)

    spread_part(e0, et_ref, 0, n_cols)
    spread_part(n0, nt_ext, MARGIN, n_cols)
    pl.semaphore_wait(barrier, len(partners))

    def gather_near(buf):
        return [
            remote(buf.at[d, mine8, :], buf.at[d, mine8, :], dev) for _, dev in near
        ]

    def gather_far(buf):
        slab = pl.ds(pl.multiple_of(yd * 8, 8), 8)
        return [remote(buf.at[slab, mine8, :], buf.at[slab, mine8, :], dev) for dev in far]

    def start(copies):
        for c in copies:
            c.start()

    def wait(copies):
        for c in copies:
            c.wait()

    north_edge = [
        remote(nt_ext.at[pl.ds(MARGIN + n_cols - 1, 1), :], nt_ext.at[pl.ds(MARGIN - 1, 1), :], at(0, 1))
    ]
    east_edge = [remote(e0.at[n_rows], e0.at[0], at(1, 0))]
    start(north_edge)
    start(east_edge)
    cond_near = gather_near(g_cond)
    start(cond_near)
    pack_copies = []
    for di, dd in around(REACH):
        lo = {0: 0, 1: 0, 2: 48, 3: 56}[abs(dd)]
        part = pl.ds(lo, PACK_ROWS - lo)
        pack_copies.append(
            remote(pack.at[1, REACH, part, :], pack.at[1 - di, REACH - dd, part, :], at(di, dd))
        )
    start(pack_copies)

    wait(north_edge)
    spread_part(n0, nt_ext, 0, MARGIN)

    wait(cond_near)
    cond_far = gather_far(g_cond)
    start(cond_far)
    wait(east_edge)

    def win(h, shift=0):
        return pl.ds(BASE[h] + shift, JP[h])

    def diagonal(h, r, shunt):
        right = N[h][r, win(h), :]
        left = N[h][r, win(h, -1), :] if h == 0 else pltpu.roll(right, 1, 0)
        return shunt + E[h][r] + E[h][r - 1] + right + left

    def stencil(h, ref, lo, hi, emit, block=8):
        def some(r0, count):
            stencil_rows(h, ref, r0, count, emit)

        full = (hi - lo) // block
        rows_loop(0, full, lambda q: some(lo + q * block, block))
        if lo + full * block < hi:
            some(lo + full * block, hi - lo - full * block)

    def stencil_rows(h, ref, r0, count, emit):
        tiles = JP[h] // 8
        for t in range(tiles):
            here = pl.ds(8 * t, 8)
            mid = pl.ds(BASE[h] + 8 * t, 8)
            below = ref[r0 - 1, mid, :]
            centre = ref[r0, mid, :]
            low = E[h][r0 - 1, here, :]
            for a in range(count):
                r = r0 + a
                above = ref[r + 1, mid, :]
                high = E[h][r, here, :]
                right = N[h][r, mid, :]
                if h == 0 or t < tiles - 1:
                    after = ref[r, pl.ds(BASE[h] + 8 * t + 1, 8), :]
                else:
                    after = pltpu.roll(centre, 7, 0)
                if h == 0 or t > 0:
                    before = ref[r, pl.ds(BASE[h] + 8 * t - 1, 8), :]
                    left = N[h][r, pl.ds(BASE[h] + 8 * t - 1, 8), :]
                else:
                    before = pltpu.roll(centre, 1, 0)
                    left = pltpu.roll(right, 1, 0)
                near = high * above + low * below + right * after + left * before
                emit(r, t, centre, near, high + low + right + left)
                below, centre, low = centre, above, high

    def set_weights(h):
        shunt = SHUNT * 4.0**h

        def fill(r):
            W[h][r] = RELAX / diagonal(h, r, shunt)

        rows_loop(1, R[h] + 2 * H[h] + 1, fill, unroll=2)

    def first(h, source=None, halo=None):
        halo = DOWNWARD[h] if halo is None else halo
        own = H[h] + 1

        def fill(r):
            if h == 0:
                s0[r - 1] = v0[slot_ref[r - 1], win(0), :] - s0[r - 1]
                U[0][r, win(0), :] = W[0][r] * s0[r - 1]
            else:
                U[h][r] = W[h][r] * (S[h] if source is None else source)[r]

        rows_loop(own - halo, own + R[h] + halo, fill, unroll=2)

    def s_tile(h, r, t, source=None):
        here = pl.ds(8 * t, 8)
        return s0[r - 1, here, :] if h == 0 else (S[h] if source is None else source)[r, here, :]

    def presmooth(h, source=None, halo=None):
        halo = max(DOWNWARD[h] - 1, 0) if halo is None else halo
        own = H[h] + 1

        def emit(r, t, centre, near, total):
            V[h][r, pl.ds(BASE[h] + 8 * t, 8), :] = W[h][r, pl.ds(8 * t, 8), :] * (
                1.2 * s_tile(h, r, t, source) + near
            )

        stencil(h, U[h], own - halo, own + R[h] + halo, emit)

    def restrict(h):
        shunt = SHUNT * 4.0**h
        grow = GROW[h]
        base = H[h] + 1 - 2 * grow
        count = R[h] + 4 * grow
        block = 8

        def pairs(q):
            held = {}
            pairs_done = {t: 0 for t in range(JP[h] // 8)}

            def emit(r, t, centre, near, total):
                value = s_tile(h, r, t) + near - (shunt + total) * centre
                if t in held:
                    first_r, first_value = held.pop(t)
                    U[h][first_r, pl.ds(BASE[h] + 8 * t, 8), :] = first_value + value
                else:
                    held[t] = (q * (block // 2) + pairs_done[t], value)
                    pairs_done[t] += 1

            stencil_rows(h, V[h], base + q * block, block, emit)

        rows_loop(0, count // block, pairs)
        cc = C[h + 1] + 2 * grow
        from_col = BASE[h] + OJ[h] - 2 * grow

        def halve(q):
            a = U[h][q, pl.ds(from_col, cc, stride=2), :]
            b = U[h][q, pl.ds(from_col + 1, cc, stride=2), :]
            if h == LEVELS - 1:
                g_src[d, pl.ds(g * 8 + q, 1), :] = a + b
            else:
                S[h + 1][q - grow + H[h + 1] + 1, pl.ds(OJ[h + 1] - grow, cc), :] = a + b

        rows_loop(0, count // 2, halve, unroll=2)

    def edges(ref):
        rows = pl.ds(1, n_rows)
        cols = pl.ds(MARGIN, n_cols)
        return [
            remote(ref.at[rows, pl.ds(MARGIN + n_cols - 1, 1), :], ref.at[rows, pl.ds(MARGIN - 1, 1), :], at(0, 1)),
            remote(ref.at[rows, pl.ds(MARGIN, 1), :], ref.at[rows, pl.ds(MARGIN + n_cols, 1), :], at(0, -1)),
            remote(ref.at[n_rows, cols, :], ref.at[0, cols, :], at(1, 0)),
            remote(ref.at[1, cols, :], ref.at[n_rows + 1, cols, :], at(-1, 0)),
        ]

    def halos(h):
        dist = -(-H[h] // C[h])
        copies = []
        for di, dd in around(dist):
            i0, ni = overlap(di, R[h], H[h])
            j0, nj = overlap(dd, C[h], H[h])
            src = S[h].at[pl.ds(i0 + H[h] + 1, ni), pl.ds(j0 + OJ[h], nj), :]
            dst = SX[h].at[
                pl.ds(i0 - di * R[h] + H[h] + 1, ni), pl.ds(j0 - dd * C[h] + OJ[h], nj), :
            ]
            copies.append(remote(src, dst, at(di, dd)))
        if SX[h] is not S[h]:
            own = (pl.ds(H[h] + 1, R[h]), pl.ds(OJ[h], C[h]))
            copies.append(
                pltpu.make_async_copy(S[h].at[own[0], own[1], :], SX[h].at[own[0], own[1], :], own_sem.at[h])
            )
        return copies

    set_weights(0)
    fetch.wait()
    fetch_table.wait()
    first(0)
    u_edges = edges(u0)
    start(u_edges)

    def spread_level(h):
        width = JP[h]
        for t, base in ((0, PACK_E[h]), (1, PACK_N[h])):
            for di in range(3):
                for dd in range(-REACH, REACH + 1):
                    first_j = dd * C[h] + OJ[h]
                    lo = max(first_j, 0)
                    hi = min(first_j + C[h], width)
                    if hi > lo and abs(dd) <= -(-(H[h] + 1) // C[h]):
                        CX[h][t, di, pl.ds(lo, hi - lo), :] = pack[
                            di, dd + REACH, pl.ds(base + lo - first_j, hi - lo), :
                        ]

        for di, lo, hi in (
            (0, R[h] - H[h] - 1, R[h]),
            (1, 0, R[h]),
            (2, 0, H[h] + 1),
        ):
            east = CX[h][0, di]
            north = CX[h][1, di]
            for i in range(lo, hi):
                r = i + H[h] + 1 + (di - 1) * R[h]
                E[h][r] = spread(east, i, JP[h])
                N[h][r] = spread(north, i, width)

        set_weights(h)

    nb = n_dev
    nn = n_grp * R[5]
    sub = iota((nn, nn), 0)
    lane = iota((nn, nn), 1)
    eye = sub == lane
    shunt5 = SHUNT * 4.0**LEVELS

    def coarse_block(k):
        both = g_cond[k]
        ee = both[:, :nn]
        low = pltpu.roll(both, 1, 0)[:, :nn]
        nc = pltpu.roll(both, 64, 1)[:, :nn]
        before = pltpu.roll(g_cond[(k - 1) % nb], 64, 1)[:, :nn]
        block = jnp.where(eye, shunt5 + ee + low + nc + before, 0.0)
        block = jnp.where(lane == sub + 1, -ee, block)
        block = jnp.where(lane == sub - 1, -low, block)
        return block, jnp.where(eye, -nc, 0.0), jnp.where(eye, -before, 0.0)

    def inverse2(a, b, c, e):
        t = 1.0 / (a * e - b * c)
        return ((e * t, -b * t), (-c * t, a * t))

    def times(m, v):
        return [m[0][0] * v[0] + m[0][1] * v[1], m[1][0] * v[0] + m[1][1] * v[1]]

    def product(m, o):
        return [[m[i][0] * o[0][j] + m[i][1] * o[1][j] for j in range(2)] for i in range(2)]

    def invert(ref):
        count = ref.shape[0]
        width = 2 if count > 8 else 4
        l3 = iota((1, nn, nn), 2)
        s3_ = iota((1, nn, nn), 1)
        lr = iota((1, 1, nn), 2)
        for k in range(0, nn, width):
            mat = ref[...]
            cols = [
                jnp.broadcast_to(mat[:, :, k + i : k + i + 1], (count, nn, nn)) for i in range(width)
            ]
            piv = [[cols[j][:, k + i : k + i + 1, :] for j in range(width)] for i in range(width)]
            rows = []
            for i in range(width):
                row = mat[:, k + i : k + i + 1, :]
                for j in range(width):
                    row = jnp.where(lr == k + j, 1.0 if i == j else 0.0, row)
                rows.append(row)
            head = inverse2(piv[0][0], piv[0][1], piv[1][0], piv[1][1])
            if width == 2:
                rows = times(head, rows)
            else:
                right = [piv[0][2:], piv[1][2:]]
                below = [piv[2][:2], piv[3][:2]]
                carried = product(below, head)
                fill = product(carried, right)
                tail = inverse2(
                    piv[2][2] - fill[0][0], piv[2][3] - fill[0][1],
                    piv[3][2] - fill[1][0], piv[3][3] - fill[1][1],
                )
                y = times(carried, rows[:2])
                low = times(tail, [rows[2] - y[0], rows[3] - y[1]])
                y = times(right, low)
                rows = times(head, [rows[0] - y[0], rows[1] - y[1]]) + low
            inside = (s3_ >= k) & (s3_ < k + width)
            new = jnp.where(inside | ((l3 >= k) & (l3 < k + width)), 0.0, mat)
            for i in range(width):
                col = jnp.where(inside, jnp.where(s3_ == k + i, -1.0, 0.0), cols[i])
                new = new - col * rows[i]
            ref[...] = new

    even = {}

    def matrices():
        even[1] = []
        for q in range(nb // 2):
            even[1].append(coarse_block(2 * q)[0])
            block, right, left = coarse_block(2 * q + 1)
            PP[1][q] = block
            MT[1][q] = jnp.concatenate([right, left], axis=0)

    def eliminate(lev):
        half = nb >> lev
        invert(PP[lev])
        zs = []
        for q in range(half):
            mt = MT[lev][q]
            inv = PP[lev][q]
            yt = dot(mt, inv)
            YT[lev][q] = yt
            YY[lev][q] = dot(inv, mt, ((1,), (1,)))
            zs.append(dot(yt, mt, ((1,), (1,))))
        new = []
        for q in range(half):
            block = even[lev][q] - zs[q][nn:, nn:]
            if q > 0:
                block = block - zs[q - 1][:nn, :nn]
            new.append(block)
        if lev == 5:
            PP[6][0] = new[0]
        else:
            for q in range(half // 2):
                odd = 2 * q + 1
                PP[lev + 1][q] = new[odd]
                MT[lev + 1][q] = jnp.concatenate(
                    [-zs[odd][:nn, nn:], -zs[odd - 1][nn:, :nn]], axis=0
                )
            even[lev + 1] = new[0::2]

    wait(pack_copies)
    for h in range(1, LEVELS):
        spread_level(h)
    wait(u_edges)
    presmooth(0)
    v_edges = edges(v0)
    start(v_edges)
    wait(cond_far)
    matrices()
    eliminate(1)
    wait(v_edges)
    restrict(0)
    def down(h):
        first(h)
        presmooth(h)
        restrict(h)

    copies = halos(1)
    start(copies)
    eliminate(2)
    eliminate(3)
    wait(copies)
    down(1)
    down(2)
    copies = halos(3)
    start(copies)
    eliminate(4)
    eliminate(5)
    wait(copies)
    late = halos(2)
    start(late)
    down(3)
    down(4)
    src_near = gather_near(g_src)
    start(src_near)
    more = halos(4)
    start(more)
    invert(PP[6])
    wait(src_near)
    src_far = gather_far(g_src)
    start(src_far)
    x_ext[...] = jnp.zeros_like(x_ext)
    for h, copies in ((2, late), (4, more)):
        wait(copies)
        first(h, SX[h], UPWARD[h] + 1)
        presmooth(h, SX[h], UPWARD[h])
    wait(src_far)

    for lev in range(1, 6):
        st = 1 << (lev - 1)
        for q in range(nb >> lev):
            odd = (2 * q + 1) * st
            upd = dot(YT[lev][q], g_src[odd])
            g_src[odd - st] = g_src[odd - st] - upd[nn:]
            if odd + st < nb:
                g_src[odd + st] = g_src[odd + st] - upd[:nn]
    inner = pl.ds(MARGIN, nn)
    x_ext[4, inner, :] = dot(PP[6][0], g_src[0])
    for lev in range(5, 0, -1):
        st = 1 << (lev - 1)
        for q in range(nb >> lev):
            odd = (2 * q + 1) * st
            x = dot(PP[lev][q], g_src[odd])
            y = YY[lev][q]
            x = x - dot(y[:, nn:], x_ext[4 + odd - st, inner, :])
            if odd + st < nb:
                x = x - dot(y[:, :nn], x_ext[4 + odd + st, inner, :])
            x_ext[4 + odd, inner, :] = x

    for k in range(8):
        part = x_ext[d + 1 + k, pl.ds(pl.multiple_of(g * 8, 8), 24), :]
        for i in range(12):
            c5[i, k : k + 1, :] = part[6 + i : 7 + i]

    def smooth(h, dst, ref, lo, hi):
        def emit(r, t, centre, near, total):
            dst[r, pl.ds(BASE[h] + 8 * t, 8), :] = 0.2 * centre + W[h][r, pl.ds(8 * t, 8), :] * (
                s_tile(h, r, t, SX[h]) + near
            )

        stencil(h, ref, lo, hi, emit)

    for h in range(LEVELS - 1, 0, -1):
        p = UPWARD[h]
        first_q = -(-p // 2)
        odd_col = OJ[h] % 2
        size = (JP[h] - odd_col) // 2

        def lift(q, h=h, size=size, odd_col=odd_col):
            if h == LEVELS - 1:
                coarse = c5[q + 2]
            else:
                cofs = OJ[h + 1] - OJ[h] // 2
                coarse = V[h + 1][q + H[h + 1] + 1, pl.ds(cofs, size), :]
            for a in range(2):
                r = 2 * q + a + H[h] + 1
                for b in range(2):
                    cols = pl.ds(odd_col + b, size, stride=2)
                    V[h][r, cols, :] = V[h][r, cols, :] + coarse

        rows_loop(-first_q, R[h] // 2 + first_q, lift, unroll=2)
        own = H[h] + 1
        smooth(h, U[h], V[h], own - (p - 1), own + R[h] + (p - 1))
        smooth(h, V[h], U[h], own - (p - 2), own + R[h] + (p - 2))

    half_cols = n_cols // 2

    def lift0(q, rows):
        coarse = V[1][q + H[1] + 1, pl.ds(OJ[1] - 1, half_cols + 2), :]
        for a in rows:
            r = 2 * q + a + 1
            for b in range(2):
                cols = pl.ds(MARGIN - 2 + b, half_cols + 2, stride=2)
                v0[r, cols, :] = v0[r, cols, :] + coarse

    lift0(-1, (1,))
    rows_loop(0, n_rows // 2, functools.partial(lift0, rows=(0, 1)), unroll=2)
    lift0(n_rows // 2, (0,))
    size = n_rows // PARTS
    order = [PARTS - 1] + list(range(PARTS - 1))
    flights = []
    cols = pl.ds(MARGIN, n_cols)
    for c in order:
        lo = 1 + c * size
        smooth(0, u0, v0, lo, lo + size)
        rows = pl.ds(lo, size)
        mine = [
            remote(u0.at[rows, pl.ds(MARGIN + n_cols - 1, 1), :], u0.at[rows, pl.ds(MARGIN - 1, 1), :], at(0, 1)),
            remote(u0.at[rows, pl.ds(MARGIN, 1), :], u0.at[rows, pl.ds(MARGIN + n_cols, 1), :], at(0, -1)),
        ]
        if c == PARTS - 1:
            last_row = remote(u0.at[n_rows, cols, :], u0.at[0, cols, :], at(1, 0))
            mine.append(last_row)
        if c == 0:
            first_row = remote(u0.at[1, cols, :], u0.at[n_rows + 1, cols, :], at(-1, 0))
            mine.append(first_row)
        start(mine)
        flights.append(mine[:2])
    done = []
    for c, mine in zip(order, flights):
        wait(mine)
        if c == PARTS - 1:
            first_row.wait()
        if c == 0:
            last_row.wait()

        def last(r, t, centre, near, total):
            here = pl.ds(8 * t, 8)
            s0[r - 1, here, :] = 0.2 * centre + w0[r, here, :] * (s0[r - 1, here, :] + near)

        stencil(0, u0, 1 + c * size, 1 + c * size + size, last)
        rows = pl.ds(c * size, size)
        done.append(pltpu.make_async_copy(s0.at[rows], out_hbm.at[rows], local.at[2 + c]))
        done[-1].start()
    wait(done)
    assert counter[0] <= N_COPIES, counter[0]


N_COPIES = 160
PARTS = 4


def body(n_grp, n_dev, load, east_class, north_class, cond_table, taps, tap_current):
    n_rows, n_cols, cands = load.shape
    slots = -(-(n_rows + 1) // TABLE_PART) * TABLE_PART
    total = n_dev * n_cols
    assert total & (total - 1) == 0
    table, slot = pl.pallas_call(
        functools.partial(tap_kernel, n_rows, n_cols, total.bit_length() - 1),
        in_specs=[pl.BlockSpec(memory_space=pltpu.VMEM)] * 2,
        out_specs=[
            pl.BlockSpec(memory_space=pl.ANY),
            pl.BlockSpec(memory_space=pltpu.SMEM),
        ],
        out_shape=[
            jax.ShapeDtypeStruct((slots, n_cols, cands), F32),
            jax.ShapeDtypeStruct((n_rows,), jnp.int32),
        ],
        scratch_shapes=[
            pltpu.VMEM((slots, n_cols, cands), F32),
            pltpu.SemaphoreType.DMA((slots // TABLE_PART,)),
        ],
        compiler_params=pltpu.CompilerParams(vmem_limit_bytes=60 << 20),
    )(taps.T, tap_current.T)

    def vm(*shape):
        return pltpu.VMEM(shape, F32)

    ext0 = (n_rows + 2, n_cols + 2 * MARGIN, LANES)
    tall = {h: (n_rows >> h) + 2 * HALO[h] + 2 for h in range(1, LEVELS)}
    levels = range(1, LEVELS)
    nn = n_dev
    scratch = [
        vm(n_rows, n_cols, LANES), vm(*ext0), vm(*ext0),
        vm(n_rows + 1, n_cols, LANES), vm(n_rows + 1, n_cols + MARGIN, LANES),
        vm(n_rows + 1, n_cols, LANES), vm(n_cols, n_rows), vm(n_cols + MARGIN, n_rows),
        vm(3, 2 * REACH + 1, PACK_ROWS, LANES),
    ]
    scratch += [vm(tall[h], WIDTH[h], LANES) for h in levels]
    scratch += [vm(tall[h], WIDTH[h], LANES) for h in levels] * 2
    scratch += [vm(tall[h], WIDTH[h], LANES) for h in levels]
    scratch += [vm(tall[h], WIDTH[h], LANES) for h in levels]
    scratch += [vm(tall[h], WIDTH[h], LANES) for h in levels]
    scratch += [vm(2, 3, WIDTH[h], LANES) for h in levels]
    scratch += [vm(tall[h], WIDTH[h], LANES) for h in (2, 4)]
    scratch += [vm(n_dev, 32, LANES), vm(n_dev, 32, LANES), vm(n_dev + 8, 32 + 16, LANES), vm(12, 8, LANES)]
    scratch += [vm(nn >> l, 64, 32) for l in range(1, 6)]
    scratch += [vm(nn >> l, 32, 64) for l in range(1, 6)]
    scratch += [vm(nn >> l, 64, 32) for l in range(1, 6)]
    scratch += [vm(nn >> l, 32, 32) for l in range(1, 6)] + [vm(1, 32, 32)]
    scratch += [
        pltpu.SemaphoreType.DMA((N_COPIES,)),
        pltpu.SemaphoreType.DMA((N_COPIES,)),
        pltpu.SemaphoreType.DMA((2 + PARTS,)),
        pltpu.SemaphoreType.DMA((LEVELS,)),
    ]
    return pl.pallas_call(
        functools.partial(cycle_kernel, n_grp, n_dev, n_rows, n_cols),
        out_shape=jax.ShapeDtypeStruct(load.shape, F32),
        in_specs=[
            pl.BlockSpec(memory_space=pl.ANY),
            pl.BlockSpec(memory_space=pl.ANY),
            pl.BlockSpec(memory_space=pltpu.SMEM),
            pl.BlockSpec(memory_space=pltpu.VMEM),
            pl.BlockSpec(memory_space=pltpu.VMEM),
            pl.BlockSpec(memory_space=pltpu.SMEM),
        ],
        out_specs=pl.BlockSpec(memory_space=pl.ANY),
        scratch_shapes=scratch,
        compiler_params=pltpu.CompilerParams(
            collective_id=0, has_side_effects=True, vmem_limit_bytes=63 << 20
        ),
    )(load, table, slot, east_class.T, north_class.T, cond_table)


def solution(mesh):
    return jax.shard_map(
        functools.partial(body, mesh.shape["grp"], mesh.shape["dev"]),
        mesh=mesh,
        in_specs=(P("grp", "dev", None), P("grp", "dev"), P("grp", "dev"), P(), P(), P()),
        out_specs=P("grp", "dev", None),
        check_vma=False,
    )
```

```python
import functools

import jax
import jax.numpy as jnp
from jax import lax
from jax.experimental import pallas as pl
from jax.experimental.pallas import tpu as pltpu
from jax.sharding import PartitionSpec as P

MESH = pl.DeviceIdType.MESH
HI = lax.Precision.HIGHEST
F32 = jnp.float32
LEVELS = 5
SHUNT = 0.01
RELAX = 0.8
LANES = 128

HALO = {1: 6, 2: 5, 3: 6, 4: 5}
WIDTH = {1: 32, 2: 24, 3: 24, 4: 16}
OFFSET = {1: 7, 2: 8, 3: 7, 4: 6}
UPWARD = {1: 3, 2: 4, 3: 4, 4: 4}
DOWNWARD = {0: 0, 1: 6, 2: 2, 3: 6, 4: 2}
GROW = {0: 0, 1: 2, 2: 0, 3: 2, 4: 0}
PACK_E = {1: 0, 2: 32, 3: 48, 4: 56}
PACK_N = {1: 16, 2: 40, 3: 52, 4: 58}
PACK_ROWS = 64
MARGIN = 8
REACH = 3
TABLE_PART = 32


def dot(a, b, dims=((1,), (0,))):
    return lax.dot_general(a, b, (dims, ((), ())), precision=HI, preferred_element_type=F32)


def iota(shape, dim):
    return lax.broadcasted_iota(jnp.int32, shape, dim)


def rows_loop(lo, hi, fn, unroll=1):
    def step(i, carry):
        fn(i)
        return carry

    lax.fori_loop(lo, hi, step, 0, unroll=unroll)


def tap_kernel(n_rows, n_cols, shift, taps_ref, cur_ref, table_hbm, slot_ref, table, sems):
    far = 1 << 24
    taps = taps_ref[...]
    cur = cur_ref[...]
    rows = jnp.right_shift(taps, shift) - lax.axis_index("grp") * n_rows
    cols = jnp.bitwise_and(taps, (1 << shift) - 1) - lax.axis_index("dev") * n_cols
    inside = (rows >= 0) & (rows < n_rows) & (cols >= 0) & (cols < n_cols)
    rows = jnp.where(inside, rows, far)
    col_ids = iota((n_cols, LANES), 0)

    def clear(i, carry):
        slot_ref[i] = 0
        return carry

    lax.fori_loop(0, n_rows, clear, 0, unroll=8)
    table[0] = jnp.zeros((n_cols, LANES), F32)

    lower = jnp.where(inside, rows, -1)

    def more(carry):
        return carry[1] <= carry[2]

    def two(carry):
        used, low, high = carry
        after = jnp.min(jnp.where(rows > low, rows, far))
        before = jnp.max(jnp.where(lower < high, lower, -1))
        for step, row in enumerate((low, high)):
            here = jnp.where(rows == row, cur, 0.0)
            total = jnp.zeros((n_cols, LANES), F32)
            for k in range(taps.shape[0]):
                total += jnp.where(cols[k : k + 1] == col_ids, here[k : k + 1], 0.0)
            table[used + step] = total
            slot_ref[row] = used + step
        return used + 2, after, before

    used, _, _ = lax.while_loop(more, two, (jnp.int32(1), jnp.min(rows), jnp.max(lower)))

    def part(c):
        at = pl.ds(c * TABLE_PART, TABLE_PART)
        return pltpu.make_async_copy(table.at[at], table_hbm.at[at], sems.at[c])

    for c in range(table.shape[0] // TABLE_PART):

        @pl.when(used > c * TABLE_PART)
        def _():
            part(c).start()

    for c in range(table.shape[0] // TABLE_PART):

        @pl.when(used > c * TABLE_PART)
        def _():
            part(c).wait()


def copy_kernel(parts, src, dst, buf, sems):
    size = src.shape[0] // parts
    rows = [pl.ds(i * size, size) for i in range(parts)]
    reads = [
        pltpu.make_async_copy(src.at[r], buf.at[r], sems.at[i]) for i, r in enumerate(rows)
    ]
    writes = [
        pltpu.make_async_copy(buf.at[r], dst.at[r], sems.at[parts + i]) for i, r in enumerate(rows)
    ]
    for c in reads:
        c.start()
    for c, w in zip(reads, writes):
        c.wait()
        w.start()
    for w in writes:
        w.wait()


def around(dist):
    return [
        (di, dd)
        for di in (-1, 0, 1)
        for dd in range(-dist, dist + 1)
        if (di, dd) != (0, 0)
    ]


def overlap(step, size, halo):
    low = max(0, step * size - halo)
    high = min(size, step * size + size + halo)
    return low, high - low


def cycle_kernel(
    n_grp, n_dev, n_rows, n_cols,
    load_hbm, table_hbm, slot_ref, east_ref, north_ref, tab_ref,
    out_hbm,
    s0, u0, v0, e0, n0, w0, et_ref, nt_ext, pack,
    s1, s2, s3, s4, u1, u2, u3, u4, v1, v2, v3, v4,
    e1, e2, e3, e4, n1, n2, n3, n4, w1, w2, w3, w4,
    cx1, cx2, cx3, cx4, sx2, sx4,
    g_cond, g_src, x_ext, c5,
    m1, m2, m3, m4, m5, y1, y2, y3, y4, y5, t1, t2, t3, t4, t5, p1, p2, p3, p4, p5, p6,
    send, recv, local, own_sem,
):
    g = lax.axis_index("grp")
    d = lax.axis_index("dev")
    S = {1: s1, 2: s2, 3: s3, 4: s4}
    U = {0: u0, 1: u1, 2: u2, 3: u3, 4: u4}
    V = {0: v0, 1: v1, 2: v2, 3: v3, 4: v4}
    E = {0: e0, 1: e1, 2: e2, 3: e3, 4: e4}
    N = {0: n0, 1: n1, 2: n2, 3: n3, 4: n4}
    W = {0: w0, 1: w1, 2: w2, 3: w3, 4: w4}
    CX = {1: cx1, 2: cx2, 3: cx3, 4: cx4}
    S[0] = s0
    SX = {0: s0, 1: s1, 2: sx2, 3: s3, 4: sx4}
    BASE = {0: MARGIN, 1: 0, 2: 0, 3: 0, 4: 0}
    MT = {1: m1, 2: m2, 3: m3, 4: m4, 5: m5}
    YY = {1: y1, 2: y2, 3: y3, 4: y4, 5: y5}
    YT = {1: t1, 2: t2, 3: t3, 4: t4, 5: t5}
    PP = {1: p1, 2: p2, 3: p3, 4: p4, 5: p5, 6: p6}
    R = {h: n_rows >> h for h in range(6)}
    C = {h: n_cols >> h for h in range(6)}
    H = dict(HALO)
    H[0] = 0
    JP = dict(WIDTH)
    JP[0] = n_cols
    OJ = dict(OFFSET)
    OJ[0] = 0

    counter = [0]

    def take():
        counter[0] += 1
        return counter[0] - 1

    def at(di, dd):
        return (lax.rem(g + (di + n_grp), n_grp), lax.rem(d + (dd + n_dev), n_dev))

    def remote(src, dst, device):
        m = take()
        return pltpu.make_async_remote_copy(
            src_ref=src, dst_ref=dst, send_sem=send.at[m], recv_sem=recv.at[m],
            device_id=device, device_id_type=MESH,
        )

    zd = lax.rem(d, 8)
    yd = d // 8
    near = [(o, (g, yd * 8 + lax.rem(zd + o, 8))) for o in range(1, 8)]
    far = [
        (lax.rem(g + a, n_grp), lax.rem(yd + b, 4) * 8 + zd)
        for a in range(n_grp)
        for b in range(4)
        if (a, b) != (0, 0)
    ]
    partners = [at(di, dd) for di, dd in around(REACH)] + [dev for _, dev in near] + far

    barrier = pltpu.get_barrier_semaphore()
    for dev in partners:
        pl.semaphore_signal(barrier, inc=1, device_id=dev, device_id_type=MESH)

    own_rows = pl.ds(0, n_rows)
    fetch = pltpu.make_async_copy(load_hbm, s0, local.at[0])
    fetch.start()
    fetch_table = pltpu.make_async_copy(
        table_hbm.at[pl.ds(0, n_rows + 1)],
        v0.at[pl.ds(0, n_rows + 1), pl.ds(MARGIN, n_cols), :],
        local.at[1],
    )
    fetch_table.start()

    def conductance(cls):
        value = jnp.full(cls.shape, tab_ref[0], F32)
        for c in range(1, 8):
            value = jnp.where(cls == c, tab_ref[c], value)
        return value

    rows_c = iota((n_cols, n_rows), 1)
    cols_c = iota((n_cols, n_rows), 0)
    et = conductance(east_ref[...])
    et = jnp.where((rows_c == n_rows - 1) & (g == n_grp - 1), 0.0, et)
    nt = conductance(north_ref[...])
    nt = jnp.where((cols_c == n_cols - 1) & (d == n_dev - 1), 0.0, nt)
    nt_ext[pl.ds(MARGIN, n_cols), :] = nt

    packed = jnp.zeros((PACK_ROWS, LANES), F32)
    ri = iota((n_rows, LANES), 0)
    li = iota((n_rows, LANES), 1)
    pr = iota((PACK_ROWS, n_cols), 0)
    pj = iota((PACK_ROWS, n_cols), 1)
    for h in range(1, LEVELS):
        f = 1 << h
        last = jnp.where(ri == li * f + (f - 1), 1.0, 0.0)
        every = jnp.where(ri // f == li, 1.0, 0.0)
        qe = dot(et, last)
        qn = dot(nt, every)
        re, rn = pr - PACK_E[h], pr - PACK_N[h]
        pick_e = jnp.where((re >= 0) & (re < C[h]) & (pj // f == re), 1.0, 0.0)
        pick_n = jnp.where((rn >= 0) & (rn < C[h]) & (pj == rn * f + (f - 1)), 1.0, 0.0)
        packed += dot(pick_e, qe) + dot(pick_n, qn)
    pack[1, REACH] = packed

    si = iota((R[5], n_rows), 0)
    ci = iota((R[5], n_rows), 1)
    fe = jnp.where(ci == si * 32 + 31, 1.0, 0.0)
    fn_ = jnp.where(ci // 32 == si, 1.0, 0.0)
    e5 = jnp.sum(dot(fe, et, ((1,), (1,))), axis=1, keepdims=True)
    n5s = dot(fn_, nt, ((1,), (1,)))
    n5 = jnp.sum(jnp.where(iota(n5s.shape, 1) == n_cols - 1, n5s, 0.0), axis=1, keepdims=True)
    both = jnp.where(iota((R[5], LANES), 1) < 64, e5, n5)
    mine8 = pl.ds(pl.multiple_of(g * 8, 8), 8)
    g_cond[d, mine8, :] = both

    def spread(block, lane, width):
        return jnp.broadcast_to(block[:, lane : lane + 1], (width, LANES))

    et_ref[...] = et

    def spread_part(dst, src, first_row, width):
        def fill(half):
            base = pl.multiple_of(half * LANES, LANES)
            blk = src[first_row : first_row + width, pl.ds(base, LANES)]
            for i in range(LANES):
                dst[base + i + 1, pl.ds(first_row, width), :] = spread(blk, i, width)

        rows_loop(0, n_rows // LANES, fill)

    spread_part(e0, et_ref, 0, n_cols)
    spread_part(n0, nt_ext, MARGIN, n_cols)
    pl.semaphore_wait(barrier, len(partners))

    def gather_near(buf):
        return [
            remote(buf.at[d, mine8, :], buf.at[d, mine8, :], dev) for _, dev in near
        ]

    def gather_far(buf):
        slab = pl.ds(pl.multiple_of(yd * 8, 8), 8)
        return [remote(buf.at[slab, mine8, :], buf.at[slab, mine8, :], dev) for dev in far]

    def start(copies):
        for c in copies:
            c.start()

    def wait(copies):
        for c in copies:
            c.wait()

    north_edge = [
        remote(nt_ext.at[pl.ds(MARGIN + n_cols - 1, 1), :], nt_ext.at[pl.ds(MARGIN - 1, 1), :], at(0, 1))
    ]
    east_edge = [remote(e0.at[n_rows], e0.at[0], at(1, 0))]
    start(north_edge)
    start(east_edge)
    cond_near = gather_near(g_cond)
    start(cond_near)
    pack_copies = []
    for di, dd in around(REACH):
        lo = {0: 0, 1: 0, 2: 48, 3: 56}[abs(dd)]
        part = pl.ds(lo, PACK_ROWS - lo)
        pack_copies.append(
            remote(pack.at[1, REACH, part, :], pack.at[1 - di, REACH - dd, part, :], at(di, dd))
        )
    start(pack_copies)

    wait(north_edge)
    spread_part(n0, nt_ext, 0, MARGIN)

    wait(cond_near)
    cond_far = gather_far(g_cond)
    start(cond_far)
    wait(east_edge)

    def win(h, shift=0):
        return pl.ds(BASE[h] + shift, JP[h])

    def diagonal(h, r, shunt):
        right = N[h][r, win(h), :]
        left = N[h][r, win(h, -1), :] if h == 0 else pltpu.roll(right, 1, 0)
        return shunt + E[h][r] + E[h][r - 1] + right + left

    def stencil(h, ref, lo, hi, emit, block=8):
        def some(r0, count):
            stencil_rows(h, ref, r0, count, emit)

        full = (hi - lo) // block
        rows_loop(0, full, lambda q: some(lo + q * block, block))
        if lo + full * block < hi:
            some(lo + full * block, hi - lo - full * block)

    def stencil_rows(h, ref, r0, count, emit):
        tiles = JP[h] // 8
        for t in range(tiles):
            here = pl.ds(8 * t, 8)
            mid = pl.ds(BASE[h] + 8 * t, 8)
            below = ref[r0 - 1, mid, :]
            centre = ref[r0, mid, :]
            low = E[h][r0 - 1, here, :]
            for a in range(count):
                r = r0 + a
                above = ref[r + 1, mid, :]
                high = E[h][r, here, :]
                right = N[h][r, mid, :]
                if h == 0 or t < tiles - 1:
                    after = ref[r, pl.ds(BASE[h] + 8 * t + 1, 8), :]
                else:
                    after = pltpu.roll(centre, 7, 0)
                if h == 0 or t > 0:
                    before = ref[r, pl.ds(BASE[h] + 8 * t - 1, 8), :]
                    left = N[h][r, pl.ds(BASE[h] + 8 * t - 1, 8), :]
                else:
                    before = pltpu.roll(centre, 1, 0)
                    left = pltpu.roll(right, 1, 0)
                near = high * above + low * below + right * after + left * before
                emit(r, t, centre, near, high + low + right + left)
                below, centre, low = centre, above, high

    def set_weights(h):
        shunt = SHUNT * 4.0**h

        def fill(r):
            W[h][r] = RELAX / diagonal(h, r, shunt)

        rows_loop(1, R[h] + 2 * H[h] + 1, fill, unroll=2)

    def first(h, source=None, halo=None):
        halo = DOWNWARD[h] if halo is None else halo
        own = H[h] + 1

        def fill(r):
            if h == 0:
                s0[r - 1] = v0[slot_ref[r - 1], win(0), :] - s0[r - 1]
                U[0][r, win(0), :] = W[0][r] * s0[r - 1]
            else:
                U[h][r] = W[h][r] * (S[h] if source is None else source)[r]

        rows_loop(own - halo, own + R[h] + halo, fill, unroll=2)

    def s_tile(h, r, t, source=None):
        here = pl.ds(8 * t, 8)
        return s0[r - 1, here, :] if h == 0 else (S[h] if source is None else source)[r, here, :]

    def presmooth(h, source=None, halo=None):
        halo = max(DOWNWARD[h] - 1, 0) if halo is None else halo
        own = H[h] + 1

        def emit(r, t, centre, near, total):
            V[h][r, pl.ds(BASE[h] + 8 * t, 8), :] = W[h][r, pl.ds(8 * t, 8), :] * (
                1.2 * s_tile(h, r, t, source) + near
            )

        stencil(h, U[h], own - halo, own + R[h] + halo, emit)

    def restrict(h):
        shunt = SHUNT * 4.0**h
        grow = GROW[h]
        base = H[h] + 1 - 2 * grow
        count = R[h] + 4 * grow
        block = 8

        def pairs(q):
            held = {}
            pairs_done = {t: 0 for t in range(JP[h] // 8)}

            def emit(r, t, centre, near, total):
                value = s_tile(h, r, t) + near - (shunt + total) * centre
                if t in held:
                    first_r, first_value = held.pop(t)
                    U[h][first_r, pl.ds(BASE[h] + 8 * t, 8), :] = first_value + value
                else:
                    held[t] = (q * (block // 2) + pairs_done[t], value)
                    pairs_done[t] += 1

            stencil_rows(h, V[h], base + q * block, block, emit)

        rows_loop(0, count // block, pairs)
        cc = C[h + 1] + 2 * grow
        from_col = BASE[h] + OJ[h] - 2 * grow

        def halve(q):
            a = U[h][q, pl.ds(from_col, cc, stride=2), :]
            b = U[h][q, pl.ds(from_col + 1, cc, stride=2), :]
            if h == LEVELS - 1:
                g_src[d, pl.ds(g * 8 + q, 1), :] = a + b
            else:
                S[h + 1][q - grow + H[h + 1] + 1, pl.ds(OJ[h + 1] - grow, cc), :] = a + b

        rows_loop(0, count // 2, halve, unroll=2)

    def edges(ref):
        rows = pl.ds(1, n_rows)
        cols = pl.ds(MARGIN, n_cols)
        return [
            remote(ref.at[rows, pl.ds(MARGIN + n_cols - 1, 1), :], ref.at[rows, pl.ds(MARGIN - 1, 1), :], at(0, 1)),
            remote(ref.at[rows, pl.ds(MARGIN, 1), :], ref.at[rows, pl.ds(MARGIN + n_cols, 1), :], at(0, -1)),
            remote(ref.at[n_rows, cols, :], ref.at[0, cols, :], at(1, 0)),
            remote(ref.at[1, cols, :], ref.at[n_rows + 1, cols, :], at(-1, 0)),
        ]

    def halos(h):
        dist = -(-H[h] // C[h])
        copies = []
        for di, dd in around(dist):
            i0, ni = overlap(di, R[h], H[h])
            j0, nj = overlap(dd, C[h], H[h])
            src = S[h].at[pl.ds(i0 + H[h] + 1, ni), pl.ds(j0 + OJ[h], nj), :]
            dst = SX[h].at[
                pl.ds(i0 - di * R[h] + H[h] + 1, ni), pl.ds(j0 - dd * C[h] + OJ[h], nj), :
            ]
            copies.append(remote(src, dst, at(di, dd)))
        if SX[h] is not S[h]:
            own = (pl.ds(H[h] + 1, R[h]), pl.ds(OJ[h], C[h]))
            copies.append(
                pltpu.make_async_copy(S[h].at[own[0], own[1], :], SX[h].at[own[0], own[1], :], own_sem.at[h])
            )
        return copies

    set_weights(0)
    fetch.wait()
    fetch_table.wait()
    first(0)
    u_edges = edges(u0)
    start(u_edges)

    def spread_level(h):
        width = JP[h]
        for t, base in ((0, PACK_E[h]), (1, PACK_N[h])):
            for di in range(3):
                for dd in range(-REACH, REACH + 1):
                    first_j = dd * C[h] + OJ[h]
                    lo = max(first_j, 0)
                    hi = min(first_j + C[h], width)
                    if hi > lo and abs(dd) <= -(-(H[h] + 1) // C[h]):
                        CX[h][t, di, pl.ds(lo, hi - lo), :] = pack[
                            di, dd + REACH, pl.ds(base + lo - first_j, hi - lo), :
                        ]

        for di, lo, hi in (
            (0, R[h] - H[h] - 1, R[h]),
            (1, 0, R[h]),
            (2, 0, H[h] + 1),
        ):
            east = CX[h][0, di]
            north = CX[h][1, di]
            for i in range(lo, hi):
                r = i + H[h] + 1 + (di - 1) * R[h]
                E[h][r] = spread(east, i, JP[h])
                N[h][r] = spread(north, i, width)

        set_weights(h)

    nb = n_dev
    nn = n_grp * R[5]
    sub = iota((nn, nn), 0)
    lane = iota((nn, nn), 1)
    eye = sub == lane
    shunt5 = SHUNT * 4.0**LEVELS

    def coarse_block(k):
        both = g_cond[k]
        ee = both[:, :nn]
        low = pltpu.roll(both, 1, 0)[:, :nn]
        nc = pltpu.roll(both, 64, 1)[:, :nn]
        before = pltpu.roll(g_cond[(k - 1) % nb], 64, 1)[:, :nn]
        block = jnp.where(eye, shunt5 + ee + low + nc + before, 0.0)
        block = jnp.where(lane == sub + 1, -ee, block)
        block = jnp.where(lane == sub - 1, -low, block)
        return block, jnp.where(eye, -nc, 0.0), jnp.where(eye, -before, 0.0)

    def inverse2(a, b, c, e):
        t = 1.0 / (a * e - b * c)
        return ((e * t, -b * t), (-c * t, a * t))

    def times(m, v):
        return [m[0][0] * v[0] + m[0][1] * v[1], m[1][0] * v[0] + m[1][1] * v[1]]

    def product(m, o):
        return [[m[i][0] * o[0][j] + m[i][1] * o[1][j] for j in range(2)] for i in range(2)]

    def invert(ref):
        count = ref.shape[0]
        width = 2 if count > 8 else 4
        l3 = iota((1, nn, nn), 2)
        s3_ = iota((1, nn, nn), 1)
        lr = iota((1, 1, nn), 2)
        for k in range(0, nn, width):
            mat = ref[...]
            cols = [
                jnp.broadcast_to(mat[:, :, k + i : k + i + 1], (count, nn, nn)) for i in range(width)
            ]
            piv = [[cols[j][:, k + i : k + i + 1, :] for j in range(width)] for i in range(width)]
            rows = []
            for i in range(width):
                row = mat[:, k + i : k + i + 1, :]
                for j in range(width):
                    row = jnp.where(lr == k + j, 1.0 if i == j else 0.0, row)
                rows.append(row)
            head = inverse2(piv[0][0], piv[0][1], piv[1][0], piv[1][1])
            if width == 2:
                rows = times(head, rows)
            else:
                right = [piv[0][2:], piv[1][2:]]
                below = [piv[2][:2], piv[3][:2]]
                carried = product(below, head)
                fill = product(carried, right)
                tail = inverse2(
                    piv[2][2] - fill[0][0], piv[2][3] - fill[0][1],
                    piv[3][2] - fill[1][0], piv[3][3] - fill[1][1],
                )
                y = times(carried, rows[:2])
                low = times(tail, [rows[2] - y[0], rows[3] - y[1]])
                y = times(right, low)
                rows = times(head, [rows[0] - y[0], rows[1] - y[1]]) + low
            inside = (s3_ >= k) & (s3_ < k + width)
            new = jnp.where(inside | ((l3 >= k) & (l3 < k + width)), 0.0, mat)
            for i in range(width):
                col = jnp.where(inside, jnp.where(s3_ == k + i, -1.0, 0.0), cols[i])
                new = new - col * rows[i]
            ref[...] = new

    even = {}

    def matrices():
        even[1] = []
        for q in range(nb // 2):
            even[1].append(coarse_block(2 * q)[0])
            block, right, left = coarse_block(2 * q + 1)
            PP[1][q] = block
            MT[1][q] = jnp.concatenate([right, left], axis=0)

    def eliminate(lev):
        half = nb >> lev
        invert(PP[lev])
        zs = []
        for q in range(half):
            mt = MT[lev][q]
            inv = PP[lev][q]
            yt = dot(mt, inv)
            YT[lev][q] = yt
            YY[lev][q] = dot(inv, mt, ((1,), (1,)))
            zs.append(dot(yt, mt, ((1,), (1,))))
        new = []
        for q in range(half):
            block = even[lev][q] - zs[q][nn:, nn:]
            if q > 0:
                block = block - zs[q - 1][:nn, :nn]
            new.append(block)
        if lev == 5:
            PP[6][0] = new[0]
        else:
            for q in range(half // 2):
                odd = 2 * q + 1
                PP[lev + 1][q] = new[odd]
                MT[lev + 1][q] = jnp.concatenate(
                    [-zs[odd][:nn, nn:], -zs[odd - 1][nn:, :nn]], axis=0
                )
            even[lev + 1] = new[0::2]

    wait(pack_copies)
    for h in range(1, LEVELS):
        spread_level(h)
    wait(u_edges)
    presmooth(0)
    v_edges = edges(v0)
    start(v_edges)
    wait(cond_far)
    matrices()
    eliminate(1)
    wait(v_edges)
    restrict(0)
    def down(h):
        first(h)
        presmooth(h)
        restrict(h)

    copies = halos(1)
    start(copies)
    eliminate(2)
    eliminate(3)
    wait(copies)
    down(1)
    down(2)
    copies = halos(3)
    start(copies)
    eliminate(4)
    eliminate(5)
    wait(copies)
    late = halos(2)
    start(late)
    down(3)
    down(4)
    src_near = gather_near(g_src)
    start(src_near)
    more = halos(4)
    start(more)
    invert(PP[6])
    wait(src_near)
    src_far = gather_far(g_src)
    start(src_far)
    x_ext[...] = jnp.zeros_like(x_ext)
    for h, copies in ((2, late), (4, more)):
        wait(copies)
        first(h, SX[h], UPWARD[h] + 1)
        presmooth(h, SX[h], UPWARD[h])
    wait(src_far)

    for lev in range(1, 6):
        st = 1 << (lev - 1)
        for q in range(nb >> lev):
            odd = (2 * q + 1) * st
            upd = dot(YT[lev][q], g_src[odd])
            g_src[odd - st] = g_src[odd - st] - upd[nn:]
            if odd + st < nb:
                g_src[odd + st] = g_src[odd + st] - upd[:nn]
    inner = pl.ds(MARGIN, nn)
    x_ext[4, inner, :] = dot(PP[6][0], g_src[0])
    for lev in range(5, 0, -1):
        st = 1 << (lev - 1)
        for q in range(nb >> lev):
            odd = (2 * q + 1) * st
            x = dot(PP[lev][q], g_src[odd])
            y = YY[lev][q]
            x = x - dot(y[:, nn:], x_ext[4 + odd - st, inner, :])
            if odd + st < nb:
                x = x - dot(y[:, :nn], x_ext[4 + odd + st, inner, :])
            x_ext[4 + odd, inner, :] = x

    for k in range(8):
        part = x_ext[d + 1 + k, pl.ds(pl.multiple_of(g * 8, 8), 24), :]
        for i in range(12):
            c5[i, k : k + 1, :] = part[6 + i : 7 + i]

    def smooth(h, dst, ref, lo, hi):
        def emit(r, t, centre, near, total):
            dst[r, pl.ds(BASE[h] + 8 * t, 8), :] = 0.2 * centre + W[h][r, pl.ds(8 * t, 8), :] * (
                s_tile(h, r, t, SX[h]) + near
            )

        stencil(h, ref, lo, hi, emit)

    for h in range(LEVELS - 1, 0, -1):
        p = UPWARD[h]
        first_q = -(-p // 2)
        odd_col = OJ[h] % 2
        size = (JP[h] - odd_col) // 2

        def lift(q, h=h, size=size, odd_col=odd_col):
            if h == LEVELS - 1:
                coarse = c5[q + 2]
            else:
                cofs = OJ[h + 1] - OJ[h] // 2
                coarse = V[h + 1][q + H[h + 1] + 1, pl.ds(cofs, size), :]
            for a in range(2):
                r = 2 * q + a + H[h] + 1
                for b in range(2):
                    cols = pl.ds(odd_col + b, size, stride=2)
                    V[h][r, cols, :] = V[h][r, cols, :] + coarse

        rows_loop(-first_q, R[h] // 2 + first_q, lift, unroll=2)
        own = H[h] + 1
        smooth(h, U[h], V[h], own - (p - 1), own + R[h] + (p - 1))
        smooth(h, V[h], U[h], own - (p - 2), own + R[h] + (p - 2))

    half_cols = n_cols // 2

    def lift0(q, rows):
        coarse = V[1][q + H[1] + 1, pl.ds(OJ[1] - 1, half_cols + 2), :]
        for a in rows:
            r = 2 * q + a + 1
            for b in range(2):
                cols = pl.ds(MARGIN - 2 + b, half_cols + 2, stride=2)
                v0[r, cols, :] = v0[r, cols, :] + coarse

    lift0(-1, (1,))
    rows_loop(0, n_rows // 2, functools.partial(lift0, rows=(0, 1)), unroll=2)
    lift0(n_rows // 2, (0,))
    size = n_rows // PARTS
    order = [PARTS - 1] + list(range(PARTS - 1))
    flights = []
    cols = pl.ds(MARGIN, n_cols)
    for c in order:
        lo = 1 + c * size
        smooth(0, u0, v0, lo, lo + size)
        rows = pl.ds(lo, size)
        mine = [
            remote(u0.at[rows, pl.ds(MARGIN + n_cols - 1, 1), :], u0.at[rows, pl.ds(MARGIN - 1, 1), :], at(0, 1)),
            remote(u0.at[rows, pl.ds(MARGIN, 1), :], u0.at[rows, pl.ds(MARGIN + n_cols, 1), :], at(0, -1)),
        ]
        if c == PARTS - 1:
            last_row = remote(u0.at[n_rows, cols, :], u0.at[0, cols, :], at(1, 0))
            mine.append(last_row)
        if c == 0:
            first_row = remote(u0.at[1, cols, :], u0.at[n_rows + 1, cols, :], at(-1, 0))
            mine.append(first_row)
        start(mine)
        flights.append(mine[:2])
    done = []
    for c, mine in zip(order, flights):
        wait(mine)
        if c == PARTS - 1:
            first_row.wait()
        if c == 0:
            last_row.wait()

        def last(r, t, centre, near, total):
            here = pl.ds(8 * t, 8)
            s0[r - 1, here, :] = 0.2 * centre + w0[r, here, :] * (s0[r - 1, here, :] + near)

        stencil(0, u0, 1 + c * size, 1 + c * size + size, last)
        rows = pl.ds(c * size, size)
        done.append(pltpu.make_async_copy(s0.at[rows], out_hbm.at[rows], local.at[2 + c]))
        done[-1].start()
    wait(done)
    assert counter[0] <= N_COPIES, counter[0]


N_COPIES = 160
PARTS = 4


def body(n_grp, n_dev, load, east_class, north_class, cond_table, taps, tap_current):
    n_rows, n_cols, cands = load.shape
    slots = -(-(n_rows + 1) // TABLE_PART) * TABLE_PART
    total = n_dev * n_cols
    assert total & (total - 1) == 0
    table, slot = pl.pallas_call(
        functools.partial(tap_kernel, n_rows, n_cols, total.bit_length() - 1),
        in_specs=[pl.BlockSpec(memory_space=pltpu.VMEM)] * 2,
        out_specs=[
            pl.BlockSpec(memory_space=pl.ANY),
            pl.BlockSpec(memory_space=pltpu.SMEM),
        ],
        out_shape=[
            jax.ShapeDtypeStruct((slots, n_cols, cands), F32),
            jax.ShapeDtypeStruct((n_rows,), jnp.int32),
        ],
        scratch_shapes=[
            pltpu.VMEM((slots, n_cols, cands), F32),
            pltpu.SemaphoreType.DMA((slots // TABLE_PART,)),
        ],
        compiler_params=pltpu.CompilerParams(vmem_limit_bytes=60 << 20),
    )(taps.T, tap_current.T)

    def vm(*shape):
        return pltpu.VMEM(shape, F32)

    ext0 = (n_rows + 2, n_cols + 2 * MARGIN, LANES)
    tall = {h: (n_rows >> h) + 2 * HALO[h] + 2 for h in range(1, LEVELS)}
    levels = range(1, LEVELS)
    nn = n_dev
    scratch = [
        vm(n_rows, n_cols, LANES), vm(*ext0), vm(*ext0),
        vm(n_rows + 1, n_cols, LANES), vm(n_rows + 1, n_cols + MARGIN, LANES),
        vm(n_rows + 1, n_cols, LANES), vm(n_cols, n_rows), vm(n_cols + MARGIN, n_rows),
        vm(3, 2 * REACH + 1, PACK_ROWS, LANES),
    ]
    scratch += [vm(tall[h], WIDTH[h], LANES) for h in levels]
    scratch += [vm(tall[h], WIDTH[h], LANES) for h in levels] * 2
    scratch += [vm(tall[h], WIDTH[h], LANES) for h in levels]
    scratch += [vm(tall[h], WIDTH[h], LANES) for h in levels]
    scratch += [vm(tall[h], WIDTH[h], LANES) for h in levels]
    scratch += [vm(2, 3, WIDTH[h], LANES) for h in levels]
    scratch += [vm(tall[h], WIDTH[h], LANES) for h in (2, 4)]
    scratch += [vm(n_dev, 32, LANES), vm(n_dev, 32, LANES), vm(n_dev + 8, 32 + 16, LANES), vm(12, 8, LANES)]
    scratch += [vm(nn >> l, 64, 32) for l in range(1, 6)]
    scratch += [vm(nn >> l, 32, 64) for l in range(1, 6)]
    scratch += [vm(nn >> l, 64, 32) for l in range(1, 6)]
    scratch += [vm(nn >> l, 32, 32) for l in range(1, 6)] + [vm(1, 32, 32)]
    scratch += [
        pltpu.SemaphoreType.DMA((N_COPIES,)),
        pltpu.SemaphoreType.DMA((N_COPIES,)),
        pltpu.SemaphoreType.DMA((2 + PARTS,)),
        pltpu.SemaphoreType.DMA((LEVELS,)),
    ]
    result = pl.pallas_call(
        functools.partial(cycle_kernel, n_grp, n_dev, n_rows, n_cols),
        out_shape=jax.ShapeDtypeStruct(load.shape, F32),
        in_specs=[
            pl.BlockSpec(memory_space=pl.ANY),
            pl.BlockSpec(memory_space=pl.ANY),
            pl.BlockSpec(memory_space=pltpu.SMEM),
            pl.BlockSpec(memory_space=pltpu.VMEM),
            pl.BlockSpec(memory_space=pltpu.VMEM),
            pl.BlockSpec(memory_space=pltpu.SMEM),
        ],
        out_specs=pl.BlockSpec(memory_space=pl.ANY),
        scratch_shapes=scratch,
        compiler_params=pltpu.CompilerParams(
            collective_id=0, has_side_effects=True, vmem_limit_bytes=63 << 20
        ),
    )(load, table, slot, east_class.T, north_class.T, cond_table)
    parts = 4
    return pl.pallas_call(
        functools.partial(copy_kernel, parts),
        out_shape=jax.ShapeDtypeStruct(load.shape, F32),
        in_specs=[pl.BlockSpec(memory_space=pl.ANY)],
        out_specs=pl.BlockSpec(memory_space=pl.ANY),
        scratch_shapes=[
            vm(n_rows, n_cols, LANES),
            pltpu.SemaphoreType.DMA((2 * parts,)),
        ],
        compiler_params=pltpu.CompilerParams(vmem_limit_bytes=60 << 20),
    )(result)


def solution(mesh):
    return jax.shard_map(
        functools.partial(body, mesh.shape["grp"], mesh.shape["dev"]),
        mesh=mesh,
        in_specs=(P("grp", "dev", None), P("grp", "dev"), P("grp", "dev"), P(), P(), P()),
        out_specs=P("grp", "dev", None),
        check_vma=False,
    )
```
